32 devices in a mesh: segment: 8 (over z, y), tp: 4 (over x, core).
Axes of the slice: x: 2, y: 2, z: 4, core: 2. Of those that a mesh axis runs over, the one named last changes fastest.
Arguments:
- residual: bfloat16 [8, 128, 4096], P('segment', 'tp'), may hold values from -6 to 6
- pending: bfloat16 [8, 128, 4096], P('segment', 'tp'), may hold values from -6 to 6
- span_index: int32 [8], P('segment'), may hold values from 0 to 63
- prefix_len: int32 [8], P('segment'), may hold values from 192 to 1536
- norm_gain: bfloat16 [8, 4096], P('segment'), may hold values from 0.099609375 to 1.8984375
- w_query: bfloat16 [8, 4096, 4096], P('segment', None, 'tp'), may hold values from -0.1875 to 0.1875
- w_kv: bfloat16 [8, 4096, 1024], P('segment', None, 'tp'), may hold values from -0.09375 to 0.09375
- w_out: bfloat16 [8, 4096, 4096], P('segment', 'tp'), may hold values from -0.5 to 0.5
- prefix_cache: bfloat16 [8, 6144, 256], P('segment', 'tp'), may hold values from -68 to 68
Outputs:
- carried: bfloat16 [8, 128, 4096], P('segment', 'tp')
- output: bfloat16 [8, 128, 4096], P('segment', 'tp')
The draws below stay inside these ranges and needn't reach their ends.
All inputs are finite; a program needn't handle non-finite values.
Results may differ from the reference program's by a relative error of at most 0.04.
Values may be sent and summed in bfloat16 or wider, within the bound.
A program may use at most 64 MiB of HBM per device.

```python
import jax
import jax.numpy as jnp
from jax import lax

D = 4096
HEADS = 32
KV_HEADS = 4
HD = 128
SPAN = 128
PREFIX = 1536
TICKS = 2
SECTIONS = 8


def draw_prefix_len(key, part):
    key = jax.random.fold_in(key, 7)
    key_base, key_high, key_low = jax.random.split(key, 3)
    lengths = jax.random.randint(key_base, (SECTIONS,), PREFIX // 8, PREFIX + 1, dtype=jnp.int32)
    high_spot = jax.random.randint(key_high, (), 0, SECTIONS, dtype=jnp.int32)
    low_spot = (high_spot + 1 + jax.random.randint(key_low, (), 0, SECTIONS - 1, dtype=jnp.int32)) % SECTIONS
    lengths = lengths.at[high_spot].set(PREFIX)
    lengths = lengths.at[low_spot].set(PREFIX // 8)
    return lengths


def draw_prefix_cache(key, part):
    key = jax.random.fold_in(key, 11)
    key_base = jax.random.fold_in(key, 0)
    shape_full = (SECTIONS, KV_HEADS * PREFIX, 2 * HD)
    return jnp.clip(jax.random.normal(key_base, shape_full, jnp.float32), -6.0, 6.0).astype(jnp.bfloat16)


def touch_ends(entries, own_key, smallest, largest):
    longest = entries.shape.index(max(entries.shape))
    spots = []
    for shift in (0, 1):
        where = [jax.random.randint(jax.random.fold_in(own_key, axis), (), 0, length) for axis, length in enumerate(entries.shape)]
        where[longest] = (where[longest] + shift) % entries.shape[longest]
        spots.append(tuple(where))
    return entries.at[spots[0]].set(smallest).at[spots[1]].set(largest)


def block_levels(stream_key, dims, pieces, smallest, high):
    def one(axis_at, blocks):
        heights = jax.random.uniform(jax.random.fold_in(jax.random.fold_in(stream_key, 6), axis_at), (blocks,), jnp.float32, smallest / len(pieces), high / len(pieces))
        return jnp.repeat(jnp.exp(heights), dims[axis_at] // blocks).reshape((-1,) + (1,) * (len(dims) - axis_at - 1))

    loudness = one(*pieces[0])
    for cut in pieces[1:]:
        loudness = loudness * one(*cut)
    return loudness


def scatter_about(own_key, shape, scale, limit, cuts=(), held_as=jnp.bfloat16):
    entries = jax.random.normal(own_key, shape, jnp.float32) * scale
    if len(cuts) > 0:
        entries = block_levels(own_key, shape, cuts, -0.22, 0.18) * entries
    return jnp.clip(entries, min=-limit, max=limit).astype(held_as)


def setup_inputs(seed: int = 0) -> dict:
    seeds = jax.random.split(jax.random.key(seed), 10)
    return {
        "residual": scatter_about(seeds[0], (SECTIONS, SPAN, D), 1.0, 6.0, ((0, 8), (1, 4))),
        "pending": scatter_about(seeds[1], (SECTIONS, SPAN, D), 1.0, 6.0, ((0, 8), (1, 4))),
        "span_index": touch_ends(jax.random.randint(seeds[2], (SECTIONS,), 0, 64), jax.random.fold_in(seeds[2], 1), 0, 63).astype(jnp.int32),
        "prefix_len": draw_prefix_len(jax.random.fold_in(seeds[9], 71), 0),
        "norm_gain": jnp.clip(1.0 + 0.18 * jax.random.normal(seeds[4], (SECTIONS, D), jnp.float32), 0.099609375, 1.8984375).astype(jnp.bfloat16),
        "w_query": scatter_about(seeds[5], (SECTIONS, D, HEADS * HD), (D // 4) ** -0.5, 0.1875, ((0, 8), (2, 4))),
        "w_kv": scatter_about(seeds[6], (SECTIONS, D, 2 * KV_HEADS * HD), D ** -0.5, 0.09375, ((0, 8), (2, 4))),
        "w_out": scatter_about(seeds[7], (SECTIONS, HEADS * HD, D), HD ** -0.5, 0.5, ((0, 8), (1, 4))),
        "prefix_cache": draw_prefix_cache(jax.random.fold_in(seeds[9], 71), 0),
    }


norm_eps = 1e-05
rope_base = 500000.0

def rotate(values, positions):
    half_width = values.shape[-1] // 2
    inverse = rope_base ** (-jnp.arange(0, values.shape[-1], 2, dtype=jnp.float32) / values.shape[-1])
    angles = positions.astype(jnp.float32)[:, None] * inverse[None, :]
    cosine_table = jnp.cos(angles)[:, None, :]
    sine_table = jnp.sin(angles)[:, None, :]
    first_half = values[..., :half_width]
    second_half = values[..., half_width:]
    return jnp.concatenate([first_half * cosine_table - second_half * sine_table, second_half * cosine_table + first_half * sine_table], axis=-1)

def section_block(section_items):
    residual_rows, pending_rows, span_number, length, gain_row, query_weight, pair_weight, out_weight, cache_rows = section_items
    widths = residual_rows.astype(jnp.float32)
    mean_square = lax.optimization_barrier(jnp.mean(widths * widths, axis=-1, keepdims=True))
    normed = (widths * lax.rsqrt(mean_square + norm_eps) * gain_row.astype(jnp.float32)).astype(jnp.bfloat16)
    positions = span_number * SPAN + jnp.arange(SPAN, dtype=jnp.int32)
    queries = jnp.dot(normed, query_weight, preferred_element_type=jnp.float32).reshape(SPAN, HEADS, HD)
    queries = rotate(queries, positions).astype(jnp.bfloat16)
    fresh_pairs = jnp.dot(normed, pair_weight, preferred_element_type=jnp.float32).astype(jnp.bfloat16)
    fresh_pairs = fresh_pairs.reshape(SPAN, KV_HEADS, 2, HD)
    new_keys = rotate(fresh_pairs[:, :, 0, :].astype(jnp.float32), positions).astype(jnp.bfloat16)
    new_values = fresh_pairs[:, :, 1, :]
    stored = cache_rows.reshape(KV_HEADS, PREFIX, 2 * HD)
    all_keys = jnp.concatenate([stored[:, :, :HD], jnp.transpose(new_keys, (1, 0, 2))], axis=1)
    all_values = jnp.concatenate([stored[:, :, HD:], jnp.transpose(new_values, (1, 0, 2))], axis=1)
    group_ratio = HEADS // KV_HEADS
    grouped = queries.reshape(SPAN, KV_HEADS, group_ratio, HD).astype(jnp.float32)
    scores = jnp.einsum('cgrd,gkd->grck', grouped, all_keys.astype(jnp.float32)) * HD ** (-0.5)
    slot_index = jnp.arange(PREFIX + SPAN, dtype=jnp.int32)[None, :]
    row_index = jnp.arange(SPAN, dtype=jnp.int32)[:, None]
    allowed = jnp.where(slot_index < PREFIX, slot_index < length, slot_index - PREFIX <= row_index)
    scores = jnp.where(allowed[None, None], scores, -jnp.inf)
    row_peak = lax.optimization_barrier(jnp.max(scores, axis=-1, keepdims=True))
    exp_scores = jnp.exp(scores - row_peak)
    denominator = lax.optimization_barrier(jnp.sum(exp_scores, axis=-1, keepdims=True))
    softmax_weights = (exp_scores / denominator).astype(jnp.bfloat16)
    attended = jnp.einsum('grck,gkd->cgrd', softmax_weights.astype(jnp.float32), all_values.astype(jnp.float32))
    attended = attended.astype(jnp.bfloat16).reshape(SPAN, HEADS * HD)
    output = jnp.dot(attended, out_weight, preferred_element_type=jnp.float32).astype(jnp.bfloat16)
    carried = (widths + pending_rows.astype(jnp.float32)).astype(jnp.bfloat16)
    return (carried, output)

def reference(residual, pending, span_index, prefix_len, norm_gain, w_query, w_kv, w_out, prefix_cache):
    for segment_tick in range(TICKS):
        carried, output = lax.map(section_block, (residual, pending, span_index, prefix_len, norm_gain, w_query, w_kv, w_out, prefix_cache))
        if segment_tick + 1 < TICKS:
            residual = jnp.concatenate([jnp.zeros_like(carried[:1]), carried[:-1]], axis=0)
            pending = jnp.concatenate([jnp.zeros_like(output[:1]), output[:-1]], axis=0)
            span_index = jnp.concatenate([jnp.zeros_like(span_index[:1]), span_index[:-1]], axis=0)
    return (carried, output)
```

```python
import functools
import math

import jax
import jax.numpy as jnp
import numpy as np
from jax import lax
from jax.experimental import pallas as pl
from jax.experimental.pallas import tpu as pltpu
from jax.sharding import PartitionSpec as P

KV_HEADS = 4
HD = 128
SPAN = 128
PREFIX = 1536
TICKS = 2


norm_eps = 1e-05
rope_base = 500000.0


def from_partner(array, axis, stride):
    return lax.ppermute(array, axis, [(i, i ^ 1 << stride) for i in range(lax.axis_size(axis))])


def shifted(block, axis, distance):
    devices = range(lax.axis_size(axis))
    route = [(i - distance, i) for i in devices if i - distance in devices]
    return lax.ppermute(block, axis, route)


def rotate(values, positions):
    half_width = values.shape[-1] // 2
    inverse = rope_base ** (
        -jnp.arange(0, values.shape[-1], 2, dtype=jnp.float32) / values.shape[-1]
    )
    angles = positions.astype(jnp.float32)[:, None] * inverse[None, :]
    cosine_table = jnp.cos(angles)[:, None, :]
    sine_table = jnp.sin(angles)[:, None, :]
    first_half = values[..., :half_width]
    second_half = values[..., half_width:]
    return jnp.concatenate(
        [
            first_half * cosine_table - second_half * sine_table,
            second_half * cosine_table + first_half * sine_table,
        ],
        axis=-1,
    )


def shards(
    residual, pending, span_index, prefix_len, norm_gain, w_query, w_kv, w_out, prefix_cache
):
    group_size = lax.axis_size("tp") // KV_HEADS
    group_bits = group_size.bit_length() - 1
    tp_place = lax.axis_index("tp")
    local_heads = w_query.shape[2] // HD
    weight_query = w_query[0]
    weight_pairs = w_kv[0]
    weight_out = w_out[0]
    query_width = weight_query.shape[1]
    gain_row = norm_gain[0].astype(jnp.float32)
    head_cache = prefix_cache[0]
    for bit_number in range(group_bits):
        partner = from_partner(head_cache, "tp", bit_number)
        lower_half = tp_place // (1 << bit_number) % 2 == 0
        head_cache = jnp.where(
            lower_half,
            jnp.concatenate([head_cache, partner], 0),
            jnp.concatenate([partner, head_cache], 0),
        )
    cache_keys = head_cache[:, :HD]
    cache_values = head_cache[:, HD:]
    slot_index = jnp.arange(PREFIX, dtype=jnp.int32)
    token_index = jnp.arange(SPAN, dtype=jnp.int32)
    causal = token_index[None, :] <= token_index[:, None]
    score_scale = HD ** (-0.5)
    rows_now = residual[0]
    pending_now = pending[0]
    index_now = span_index
    for segment_tick in range(TICKS):
        last_tick = segment_tick + 1 == TICKS
        widths = rows_now.astype(jnp.float32)
        mean_square = jnp.mean(widths * widths, axis=-1, keepdims=True)
        normed = (widths * lax.rsqrt(mean_square + norm_eps) * gain_row).astype(jnp.bfloat16)
        carried = (widths + pending_now.astype(jnp.float32)).astype(jnp.bfloat16)
        block_rows = lax.all_gather(normed, "tp", axis=0, tiled=True)
        projected = jnp.concatenate(
            [
                jnp.dot(block_rows, weight_query, preferred_element_type=jnp.float32),
                jnp.dot(block_rows, weight_pairs, preferred_element_type=jnp.float32),
            ],
            axis=1,
        )
        positions = index_now[0] * SPAN + token_index
        queries = rotate(
            projected[:, :query_width].reshape(SPAN, local_heads, HD), positions
        ).astype(jnp.bfloat16)
        fresh_head = projected[:, query_width:].astype(jnp.bfloat16)
        for bit_number in range(group_bits):
            partner = from_partner(fresh_head, "tp", bit_number)
            lower_half = tp_place // (1 << bit_number) % 2 == 0
            fresh_head = jnp.where(
                lower_half,
                jnp.concatenate([fresh_head, partner], 1),
                jnp.concatenate([partner, fresh_head], 1),
            )
        new_keys = rotate(fresh_head[:, None, :HD].astype(jnp.float32), positions)[:, 0, :].astype(
            jnp.bfloat16
        )
        new_values = fresh_head[:, HD:]
        score_prefix = (
            jnp.einsum("chd,pd->hcp", queries, cache_keys, preferred_element_type=jnp.float32)
            * score_scale
        )
        score_span = (
            jnp.einsum("chd,kd->hck", queries, new_keys, preferred_element_type=jnp.float32)
            * score_scale
        )
        score_prefix = jnp.where(
            (slot_index < prefix_len[0])[None, None, :], score_prefix, -jnp.inf
        )
        score_span = jnp.where(causal[None], score_span, -jnp.inf)
        row_peak = jnp.maximum(
            jnp.max(score_prefix, axis=-1, keepdims=True),
            jnp.max(score_span, axis=-1, keepdims=True),
        )
        exp_prefix = jnp.exp(score_prefix - row_peak)
        exp_span = jnp.exp(score_span - row_peak)
        denominator = jnp.sum(exp_prefix, axis=-1, keepdims=True) + jnp.sum(
            exp_span, axis=-1, keepdims=True
        )
        weight_prefix = (exp_prefix / denominator).astype(jnp.bfloat16)
        weight_span = (exp_span / denominator).astype(jnp.bfloat16)
        attended = jnp.einsum(
            "hcp,pd->chd", weight_prefix, cache_values, preferred_element_type=jnp.float32
        )
        attended = attended + jnp.einsum(
            "hck,kd->chd", weight_span, new_values, preferred_element_type=jnp.float32
        )
        attended = attended.astype(jnp.bfloat16).reshape(SPAN, local_heads * HD)
        summed = lax.psum_scatter(
            jnp.dot(attended, weight_out, preferred_element_type=jnp.float32),
            "tp",
            scatter_dimension=0,
            tiled=True,
        )
        output = summed.astype(jnp.bfloat16)
        if not last_tick:
            rows_now, pending_now, index_now = shifted((carried, output, index_now), "segment", 1)
    return (carried[None], output[None])


TP = 4
ROWS = SPAN // TP
HALF = ROWS // 2
OUT_CHUNKS = 4
TILE = 256
MASKED = -1e30


def fused_kernel(
    sections,
    span_ref,
    len_ref,
    residual_ref,
    pending_ref,
    gain_ref,
    inverse_ref,
    w_query_hbm,
    w_kv_hbm,
    w_out_hbm,
    cache_hbm,
    carried_ref,
    output_ref,
    w_query,
    w_kv,
    w_out,
    keys,
    values,
    tokens,
    carried_own,
    carried_in,
    index_own,
    index_in,
    projected,
    queries,
    attended,
    partial,
    own_sum,
    pair_send,
    pair_recv,
    far_send,
    far_recv,
    first_out,
    out_in,
    load_sem,
    gather_send,
    gather_recv,
    shift_send,
    shift_recv,
    pair_send_sem,
    pair_recv_sem,
    far_send_sem,
    far_recv_sem,
    out_send_sem,
    out_recv_sem,
):
    features = w_query.shape[0]
    query_width = w_query.shape[1]
    heads = query_width // HD
    chunk = features // OUT_CHUNKS
    seg = lax.axis_index("segment")
    me = lax.axis_index("tp")
    pair = me + 1 - 2 * lax.rem(me, 2)
    far = lax.rem(me + 2, TP)
    far_pair = lax.rem(pair + 2, TP)
    has_prev = seg > 0
    has_next = seg < sections - 1

    loads = []
    quarter = features // 4
    for part in range(4):
        span = pl.ds(part * quarter, quarter)
        loads.append((w_query_hbm.at[0, span], w_query.at[span]))
    loads.append((w_kv_hbm.at[0], w_kv))
    loads.append((cache_hbm.at[0, :, pl.ds(0, HD)], keys.at[pl.ds(0, PREFIX)]))
    loads.append((cache_hbm.at[0, :, pl.ds(HD, HD)], values.at[pl.ds(0, PREFIX)]))
    quarter_out = query_width // 4
    for part in range(4):
        span = pl.ds(part * quarter_out, quarter_out)
        loads.append((w_out_hbm.at[0, span], w_out.at[span]))
    loads = [
        pltpu.make_async_copy(source, target, load_sem.at[number])
        for number, (source, target) in enumerate(loads)
    ]
    for load in loads:
        load.start()

    barrier = pltpu.get_barrier_semaphore()
    for partner in (pair, far):
        pl.semaphore_signal(barrier, inc=1, device_id={"tp": partner})

    @pl.when(has_prev)
    def _():
        pl.semaphore_signal(barrier, inc=1, device_id={"segment": seg - 1})

    @pl.when(has_next)
    def _():
        pl.semaphore_signal(barrier, inc=1, device_id={"segment": seg + 1})

    gain = gain_ref[...].astype(jnp.float32)

    def rows_of(rank, part=None):
        if part is None:
            return pl.ds(pl.multiple_of(rank * ROWS, ROWS), ROWS)
        return pl.ds(pl.multiple_of(rank * ROWS + part * HALF, HALF), HALF)

    def normed(rows):
        widths = rows.astype(jnp.float32)
        mean_square = jnp.mean(widths * widths, axis=-1, keepdims=True)
        return (widths * lax.rsqrt(mean_square + norm_eps) * gain).astype(jnp.bfloat16)

    def gather_copy(tick, leg, part):
        rank = far if leg == 2 else me
        block = tokens.at[tick, rows_of(rank, part)]
        return pltpu.make_async_remote_copy(
            src_ref=block,
            dst_ref=block,
            send_sem=gather_send.at[tick, leg, part],
            recv_sem=gather_recv.at[tick, leg, part],
            device_id={"tp": far if leg == 0 else pair},
        )

    def shift_copy(part):
        rows = pl.ds(part * HALF, HALF)
        return pltpu.make_async_remote_copy(
            src_ref=carried_own.at[rows],
            dst_ref=carried_in.at[rows],
            send_sem=shift_send.at[part],
            recv_sem=shift_recv.at[part],
            device_id={"segment": seg + 1},
        )

    def index_copy():
        return pltpu.make_async_remote_copy(
            src_ref=index_own,
            dst_ref=index_in,
            send_sem=shift_send.at[2],
            recv_sem=shift_recv.at[2],
            device_id={"segment": seg + 1},
        )

    def pair_copy(tick, number):
        return pltpu.make_async_remote_copy(
            src_ref=pair_send.at[tick, number],
            dst_ref=pair_recv.at[tick, number],
            send_sem=pair_send_sem.at[tick, number],
            recv_sem=pair_recv_sem.at[tick, number],
            device_id={"tp": pair},
        )

    def far_copy(tick, number):
        return pltpu.make_async_remote_copy(
            src_ref=far_send.at[tick, number],
            dst_ref=far_recv.at[tick, number],
            send_sem=far_send_sem.at[tick, number],
            recv_sem=far_recv_sem.at[tick, number],
            device_id={"tp": far},
        )

    def out_copy(number):
        return pltpu.make_async_remote_copy(
            src_ref=first_out.at[number],
            dst_ref=out_in.at[number],
            send_sem=out_send_sem.at[number],
            recv_sem=out_recv_sem.at[number],
            device_id={"segment": seg + 1},
        )

    tokens[0, rows_of(me)] = normed(residual_ref[0])
    carried_own[...] = (
        residual_ref[0].astype(jnp.float32) + pending_ref[0].astype(jnp.float32)
    ).astype(jnp.bfloat16)
    index_own[...] = jnp.full(index_own.shape, span_ref[0], jnp.int32)

    pl.semaphore_wait(barrier, 2 + has_prev.astype(jnp.int32) + has_next.astype(jnp.int32))

    for part in range(2):
        gather_copy(0, 0, part).start()

    @pl.when(has_next)
    def _():
        for part in range(2):
            shift_copy(part).start()
        index_copy().start()

    for part in range(2):
        gather_copy(0, 1, part).start()

    @pl.when(jnp.logical_not(has_prev))
    def _():
        carried_in[...] = jnp.zeros_like(carried_in)
        index_in[...] = jnp.zeros_like(index_in)
        out_in[...] = jnp.zeros_like(out_in)

    lane = lax.broadcasted_iota(jnp.int32, (SPAN, HD), 1)
    row = lax.broadcasted_iota(jnp.int32, (SPAN, HD), 0)

    def tables(index_tile):
        positions = (index_tile[0:1, :] * SPAN + row).astype(jnp.float32)
        angles = positions * inverse_ref[0:1, :]
        sine = jnp.sin(angles)
        return jnp.cos(angles), jnp.where(lane < HD // 2, -sine, sine)

    def rotated(block, table):
        cosine, sine = table
        return (block * cosine + pltpu.roll(block, HD // 2, 1) * sine).astype(jnp.bfloat16)

    causal_bias = jnp.where(lane <= row, 0.0, MASKED).astype(jnp.float32)
    group = TILE // SPAN
    causal_bias = jnp.concatenate([causal_bias] * group, 0)
    slot = lax.broadcasted_iota(jnp.int32, (1, PREFIX), 1)
    slot_bias = jnp.where(slot < len_ref[0], 0.0, MASKED).astype(jnp.float32)
    score_scale = HD ** (-0.5) * math.log2(math.e)

    table = tables(index_own[...])

    for part in range(2):
        gather_copy(0, 0, part).wait_recv()
        gather_copy(0, 2, part).start()

        @pl.when(has_prev)
        def _():
            shift_copy(part).wait_recv()

        tokens[1, rows_of(me, part)] = normed(carried_in[part * HALF : (part + 1) * HALF])
        gather_copy(1, 0, part).start()
        gather_copy(1, 1, part).start()

    def project(tick):
        def tile(number, carry):
            columns = pl.ds(pl.multiple_of(number * TILE, TILE), TILE)
            projected[:, columns] = jnp.dot(
                tokens[tick], w_query[:, columns], preferred_element_type=jnp.float32
            )
            return carry

        lax.fori_loop(0, query_width // TILE, tile, 0)
        projected[:, query_width:] = jnp.dot(
            tokens[tick], w_kv[...], preferred_element_type=jnp.float32
        )

    def attend(table):
        for head in range(heads):
            block = projected[:, head * HD : (head + 1) * HD]
            queries[head * SPAN : (head + 1) * SPAN] = rotated(block, table)
        fresh_key = projected[:, query_width : query_width + HD].astype(jnp.bfloat16)
        keys[PREFIX:] = rotated(fresh_key.astype(jnp.float32), table)
        values[PREFIX:] = projected[:, query_width + HD :].astype(jnp.bfloat16)
        transposed = (((1,), (1,)), ((), ()))
        for block in range(heads // group):
            query = queries[block * TILE : (block + 1) * TILE]
            prefix = lax.dot_general(
                query, keys[:PREFIX], transposed, preferred_element_type=jnp.float32
            )
            fresh = lax.dot_general(
                query, keys[PREFIX:], transposed, preferred_element_type=jnp.float32
            )
            prefix = prefix * score_scale + slot_bias
            fresh = fresh * score_scale + causal_bias
            peak = jnp.maximum(
                jnp.max(prefix, axis=-1, keepdims=True), jnp.max(fresh, axis=-1, keepdims=True)
            )
            prefix = jnp.exp2(prefix - peak)
            fresh = jnp.exp2(fresh - peak)
            total = jnp.sum(prefix, axis=-1, keepdims=True) + jnp.sum(
                fresh, axis=-1, keepdims=True
            )
            mixed = jnp.dot(
                prefix.astype(jnp.bfloat16), values[:PREFIX], preferred_element_type=jnp.float32
            ) + jnp.dot(
                fresh.astype(jnp.bfloat16), values[PREFIX:], preferred_element_type=jnp.float32
            )
            mixed = (mixed / total).astype(jnp.bfloat16)
            for place in range(group):
                head = block * group + place
                attended[:, head * HD : (head + 1) * HD] = mixed[place * SPAN : (place + 1) * SPAN]

    def pass_on(tick, number):
        columns = slice(number * chunk, (number + 1) * chunk)
        pair_copy(tick, number).wait_recv()
        far_send[tick, number] = (
            partial[rows_of(far), columns] + pair_recv[tick, number, 1].astype(jnp.float32)
        ).astype(jnp.bfloat16)
        far_copy(tick, number).start()
        own_sum[tick, :, columns] = partial[rows_of(me), columns] + pair_recv[
            tick, number, 0
        ].astype(jnp.float32)

    def emit(tick):
        for number in range(OUT_CHUNKS):
            columns = slice(number * chunk, (number + 1) * chunk)

            def tile(step, carry):
                place = pl.ds(pl.multiple_of(number * chunk + step * TILE, TILE), TILE)
                partial[:, place] = jnp.dot(
                    attended[...], w_out[:, place], preferred_element_type=jnp.float32
                )
                return carry

            lax.fori_loop(0, chunk // TILE, tile, 0)
            pair_send[tick, number, 0] = partial[rows_of(pair), columns].astype(jnp.bfloat16)
            pair_send[tick, number, 1] = partial[rows_of(far_pair), columns].astype(jnp.bfloat16)
            pair_copy(tick, number).start()
            if number > 0:
                pass_on(tick, number - 1)
        pass_on(tick, OUT_CHUNKS - 1)

    def summed(tick, number):
        columns = slice(number * chunk, (number + 1) * chunk)
        far_copy(tick, number).wait_recv()
        return (own_sum[tick, :, columns] + far_recv[tick, number].astype(jnp.float32)).astype(
            jnp.bfloat16
        )

    for part in range(2):
        for leg in (1, 2):
            gather_copy(0, leg, part).wait_recv()
    for load in loads[:5]:
        load.wait()
    project(0)
    for part in range(2):
        gather_copy(1, 0, part).wait_recv()
        gather_copy(1, 2, part).start()
    for load in loads[5:]:
        load.wait()
    attend(table)
    emit(0)

    for part in range(2):
        for leg in (1, 2):
            gather_copy(1, leg, part).wait_recv()
    project(1)

    @pl.when(has_prev)
    def _():
        index_copy().wait_recv()

    attend(tables(index_in[...]))
    for number in range(OUT_CHUNKS):
        first_out[number] = summed(0, number)

        @pl.when(has_next)
        def _():
            out_copy(number).start()

    emit(1)
    for number in range(OUT_CHUNKS):
        columns = slice(number * chunk, (number + 1) * chunk)

        @pl.when(has_prev)
        def _():
            out_copy(number).wait_recv()

        carried_ref[0, :, columns] = (
            carried_in[:, columns].astype(jnp.float32) + out_in[number].astype(jnp.float32)
        ).astype(jnp.bfloat16)
    for number in range(OUT_CHUNKS):
        columns = slice(number * chunk, (number + 1) * chunk)
        output_ref[0, :, columns] = summed(1, number)

    for tick in range(2):
        for part in range(2):
            for leg in range(3):
                gather_copy(tick, leg, part).wait_send()
        for number in range(OUT_CHUNKS):
            pair_copy(tick, number).wait_send()
            far_copy(tick, number).wait_send()

    @pl.when(has_next)
    def _():
        for part in range(2):
            shift_copy(part).wait_send()
        index_copy().wait_send()
        for number in range(OUT_CHUNKS):
            out_copy(number).wait_send()


def fused(
    sections,
    residual,
    pending,
    span_index,
    prefix_len,
    norm_gain,
    w_query,
    w_kv,
    w_out,
    prefix_cache,
):
    features, query_width = w_query.shape[1:]
    pair_width = w_kv.shape[2]
    chunk = features // OUT_CHUNKS
    exponents = -np.arange(0, HD, 2, dtype=np.float64) / HD
    inverse = np.tile((rope_base**exponents).astype(np.float32), 2)
    inverse = jnp.asarray(np.tile(inverse[None], (8, 1)))
    smem = pl.BlockSpec(memory_space=pltpu.SMEM)
    vmem = pl.BlockSpec(memory_space=pltpu.VMEM)
    whole = pl.BlockSpec(memory_space=pl.ANY)
    half = jnp.bfloat16
    dma = pltpu.SemaphoreType.DMA
    return pl.pallas_call(
        functools.partial(fused_kernel, sections),
        out_shape=(
            jax.ShapeDtypeStruct(residual.shape, half),
            jax.ShapeDtypeStruct(residual.shape, half),
        ),
        in_specs=[smem, smem, vmem, vmem, vmem, vmem, whole, whole, whole, whole],
        out_specs=(vmem, vmem),
        scratch_shapes=[
            pltpu.VMEM((features, query_width), half),
            pltpu.VMEM((features, pair_width), half),
            pltpu.VMEM((query_width, features), half),
            pltpu.VMEM((PREFIX + SPAN, HD), half),
            pltpu.VMEM((PREFIX + SPAN, HD), half),
            pltpu.VMEM((2, SPAN, features), half),
            pltpu.VMEM((ROWS, features), half),
            pltpu.VMEM((ROWS, features), half),
            pltpu.VMEM((8, HD), jnp.int32),
            pltpu.VMEM((8, HD), jnp.int32),
            pltpu.VMEM((SPAN, query_width + pair_width), jnp.float32),
            pltpu.VMEM((query_width // HD * SPAN, HD), half),
            pltpu.VMEM((SPAN, query_width), half),
            pltpu.VMEM((SPAN, features), jnp.float32),
            pltpu.VMEM((2, ROWS, features), jnp.float32),
            pltpu.VMEM((2, OUT_CHUNKS, 2, ROWS, chunk), half),
            pltpu.VMEM((2, OUT_CHUNKS, 2, ROWS, chunk), half),
            pltpu.VMEM((2, OUT_CHUNKS, ROWS, chunk), half),
            pltpu.VMEM((2, OUT_CHUNKS, ROWS, chunk), half),
            pltpu.VMEM((OUT_CHUNKS, ROWS, chunk), half),
            pltpu.VMEM((OUT_CHUNKS, ROWS, chunk), half),
            dma((11,)),
            dma((2, 3, 2)),
            dma((2, 3, 2)),
            dma((3,)),
            dma((3,)),
            dma((2, OUT_CHUNKS)),
            dma((2, OUT_CHUNKS)),
            dma((2, OUT_CHUNKS)),
            dma((2, OUT_CHUNKS)),
            dma((OUT_CHUNKS,)),
            dma((OUT_CHUNKS,)),
        ],
        compiler_params=pltpu.CompilerParams(
            collective_id=0, has_side_effects=True, vmem_limit_bytes=56 * 1024 * 1024
        ),
        name="fused_relay",
    )(
        span_index,
        prefix_len,
        residual,
        pending,
        norm_gain,
        inverse,
        w_query,
        w_kv,
        w_out,
        prefix_cache,
    )


def solution(mesh):
    in_specs = (
        P("segment", "tp", None),
        P("segment", "tp", None),
        P("segment"),
        P("segment"),
        P("segment", None),
        P("segment", None, "tp"),
        P("segment", None, "tp"),
        P("segment", "tp", None),
        P("segment", "tp", None),
    )
    out_specs = (P("segment", "tp", None), P("segment", "tp", None))
    body = shards
    if mesh.shape["tp"] == TP == KV_HEADS and TICKS == 2:
        body = functools.partial(fused, mesh.shape["segment"])
    return jax.shard_map(body, mesh=mesh, in_specs=in_specs, out_specs=out_specs, check_vma=False)
```

```python
import functools
import math

import jax
import jax.numpy as jnp
import numpy as np
from jax import lax
from jax.experimental import pallas as pl
from jax.experimental.pallas import tpu as pltpu
from jax.sharding import PartitionSpec as P

KV_HEADS = 4
HD = 128
SPAN = 128
PREFIX = 1536
TICKS = 2


norm_eps = 1e-05
rope_base = 500000.0


def from_partner(array, axis, stride):
    return lax.ppermute(array, axis, [(i, i ^ 1 << stride) for i in range(lax.axis_size(axis))])


def shifted(block, axis, distance):
    devices = range(lax.axis_size(axis))
    route = [(i - distance, i) for i in devices if i - distance in devices]
    return lax.ppermute(block, axis, route)


def rotate(values, positions):
    half_width = values.shape[-1] // 2
    inverse = rope_base ** (
        -jnp.arange(0, values.shape[-1], 2, dtype=jnp.float32) / values.shape[-1]
    )
    angles = positions.astype(jnp.float32)[:, None] * inverse[None, :]
    cosine_table = jnp.cos(angles)[:, None, :]
    sine_table = jnp.sin(angles)[:, None, :]
    first_half = values[..., :half_width]
    second_half = values[..., half_width:]
    return jnp.concatenate(
        [
            first_half * cosine_table - second_half * sine_table,
            second_half * cosine_table + first_half * sine_table,
        ],
        axis=-1,
    )


def shards(
    residual, pending, span_index, prefix_len, norm_gain, w_query, w_kv, w_out, prefix_cache
):
    group_size = lax.axis_size("tp") // KV_HEADS
    group_bits = group_size.bit_length() - 1
    tp_place = lax.axis_index("tp")
    local_heads = w_query.shape[2] // HD
    weight_query = w_query[0]
    weight_pairs = w_kv[0]
    weight_out = w_out[0]
    query_width = weight_query.shape[1]
    gain_row = norm_gain[0].astype(jnp.float32)
    head_cache = prefix_cache[0]
    for bit_number in range(group_bits):
        partner = from_partner(head_cache, "tp", bit_number)
        lower_half = tp_place // (1 << bit_number) % 2 == 0
        head_cache = jnp.where(
            lower_half,
            jnp.concatenate([head_cache, partner], 0),
            jnp.concatenate([partner, head_cache], 0),
        )
    cache_keys = head_cache[:, :HD]
    cache_values = head_cache[:, HD:]
    slot_index = jnp.arange(PREFIX, dtype=jnp.int32)
    token_index = jnp.arange(SPAN, dtype=jnp.int32)
    causal = token_index[None, :] <= token_index[:, None]
    score_scale = HD ** (-0.5)
    rows_now = residual[0]
    pending_now = pending[0]
    index_now = span_index
    for segment_tick in range(TICKS):
        last_tick = segment_tick + 1 == TICKS
        widths = rows_now.astype(jnp.float32)
        mean_square = jnp.mean(widths * widths, axis=-1, keepdims=True)
        normed = (widths * lax.rsqrt(mean_square + norm_eps) * gain_row).astype(jnp.bfloat16)
        carried = (widths + pending_now.astype(jnp.float32)).astype(jnp.bfloat16)
        block_rows = lax.all_gather(normed, "tp", axis=0, tiled=True)
        projected = jnp.concatenate(
            [
                jnp.dot(block_rows, weight_query, preferred_element_type=jnp.float32),
                jnp.dot(block_rows, weight_pairs, preferred_element_type=jnp.float32),
            ],
            axis=1,
        )
        positions = index_now[0] * SPAN + token_index
        queries = rotate(
            projected[:, :query_width].reshape(SPAN, local_heads, HD), positions
        ).astype(jnp.bfloat16)
        fresh_head = projected[:, query_width:].astype(jnp.bfloat16)
        for bit_number in range(group_bits):
            partner = from_partner(fresh_head, "tp", bit_number)
            lower_half = tp_place // (1 << bit_number) % 2 == 0
            fresh_head = jnp.where(
                lower_half,
                jnp.concatenate([fresh_head, partner], 1),
                jnp.concatenate([partner, fresh_head], 1),
            )
        new_keys = rotate(fresh_head[:, None, :HD].astype(jnp.float32), positions)[:, 0, :].astype(
            jnp.bfloat16
        )
        new_values = fresh_head[:, HD:]
        score_prefix = (
            jnp.einsum("chd,pd->hcp", queries, cache_keys, preferred_element_type=jnp.float32)
            * score_scale
        )
        score_span = (
            jnp.einsum("chd,kd->hck", queries, new_keys, preferred_element_type=jnp.float32)
            * score_scale
        )
        score_prefix = jnp.where(
            (slot_index < prefix_len[0])[None, None, :], score_prefix, -jnp.inf
        )
        score_span = jnp.where(causal[None], score_span, -jnp.inf)
        row_peak = jnp.maximum(
            jnp.max(score_prefix, axis=-1, keepdims=True),
            jnp.max(score_span, axis=-1, keepdims=True),
        )
        exp_prefix = jnp.exp(score_prefix - row_peak)
        exp_span = jnp.exp(score_span - row_peak)
        denominator = jnp.sum(exp_prefix, axis=-1, keepdims=True) + jnp.sum(
            exp_span, axis=-1, keepdims=True
        )
        weight_prefix = (exp_prefix / denominator).astype(jnp.bfloat16)
        weight_span = (exp_span / denominator).astype(jnp.bfloat16)
        attended = jnp.einsum(
            "hcp,pd->chd", weight_prefix, cache_values, preferred_element_type=jnp.float32
        )
        attended = attended + jnp.einsum(
            "hck,kd->chd", weight_span, new_values, preferred_element_type=jnp.float32
        )
        attended = attended.astype(jnp.bfloat16).reshape(SPAN, local_heads * HD)
        summed = lax.psum_scatter(
            jnp.dot(attended, weight_out, preferred_element_type=jnp.float32),
            "tp",
            scatter_dimension=0,
            tiled=True,
        )
        output = summed.astype(jnp.bfloat16)
        if not last_tick:
            rows_now, pending_now, index_now = shifted((carried, output, index_now), "segment", 1)
    return (carried[None], output[None])


TP = 4
ROWS = SPAN // TP
HALF = 2 * ROWS
PIECE = ROWS // 2
OUT_CHUNKS = 4
TILE = 256
WIDE = 512
MASKED = -1e30


def fused_kernel(
    sections,
    span_ref,
    len_ref,
    residual_hbm,
    pending_hbm,
    gain_ref,
    inverse_ref,
    w_query_hbm,
    w_kv_hbm,
    w_out_hbm,
    cache_hbm,
    carried_ref,
    output_ref,
    residual,
    pending,
    w_query,
    w_kv,
    w_out,
    keys,
    values,
    span_keys,
    span_values,
    tokens,
    carried_own,
    carried_in,
    index_own,
    index_in,
    cosines,
    sines,
    projected,
    queries,
    peaks,
    totals,
    mixes,
    attended,
    partial,
    pair_send,
    pair_recv,
    far_send,
    far_recv,
    first_out,
    out_in,
    row_sem,
    load_sem,
    gather_send,
    gather_recv,
    shift_send,
    shift_recv,
    pair_send_sem,
    pair_recv_sem,
    far_send_sem,
    far_recv_sem,
    out_send_sem,
    out_recv_sem,
):
    features = w_query.shape[0]
    query_width = w_query.shape[1]
    heads = query_width // HD
    chunk = features // OUT_CHUNKS
    seg = lax.axis_index("segment")
    me = lax.axis_index("tp")
    core = lax.rem(me, 2)
    side = me // 2
    pair = me + 1 - 2 * core
    far = lax.rem(me + 2, TP)
    has_prev = seg > 0
    has_next = seg < sections - 1

    barrier = pltpu.get_barrier_semaphore()
    for partner in (pair, far):
        pl.semaphore_signal(barrier, inc=1, device_id={"tp": partner})

    @pl.when(has_prev)
    def _():
        pl.semaphore_signal(barrier, inc=1, device_id={"segment": seg - 1})

    @pl.when(has_next)
    def _():
        pl.semaphore_signal(barrier, inc=1, device_id={"segment": seg + 1})

    row_loads = [
        pltpu.make_async_copy(residual_hbm.at[0], residual, row_sem.at[0]),
        pltpu.make_async_copy(pending_hbm.at[0], pending, row_sem.at[1]),
    ]
    loads = []
    quarter = features // 4
    for part in range(4):
        span = pl.ds(part * quarter, quarter)
        loads.append((w_query_hbm.at[0, span], w_query.at[span]))
    loads.append((w_kv_hbm.at[0], w_kv))
    loads.append((cache_hbm.at[0, :, pl.ds(0, HD)], keys))
    loads.append((cache_hbm.at[0, :, pl.ds(HD, HD)], values))
    quarter_out = query_width // 4
    for part in range(4):
        span = pl.ds(part * quarter_out, quarter_out)
        loads.append((w_out_hbm.at[0, span], w_out.at[span]))
    loads = [
        pltpu.make_async_copy(source, target, load_sem.at[number])
        for number, (source, target) in enumerate(loads)
    ]
    for load in row_loads + loads:
        load.start()

    gain = gain_ref[...].astype(jnp.float32)

    def rows_of(slot, which, part=None):
        if part is None:
            return pl.ds(pl.multiple_of(slot * HALF + which * ROWS, ROWS), ROWS)
        return pl.ds(pl.multiple_of(slot * HALF + which * ROWS + part * PIECE, PIECE), PIECE)

    def normed(rows):
        widths = rows.astype(jnp.float32)
        mean_square = jnp.mean(widths * widths, axis=-1, keepdims=True)
        return (widths * lax.rsqrt(mean_square + norm_eps) * gain).astype(jnp.bfloat16)

    def gather_copy(tick, leg, part):
        here, there = ((0, 1), (0, 0), (1, 1))[leg]
        return pltpu.make_async_remote_copy(
            src_ref=tokens.at[rows_of(2 * tick + here, core, part)],
            dst_ref=tokens.at[rows_of(2 * tick + there, core, part)],
            send_sem=gather_send.at[tick, leg, part],
            recv_sem=gather_recv.at[tick, leg, part],
            device_id={"tp": far if leg == 0 else pair},
        )

    def shift_copy(part):
        rows = pl.ds(part * PIECE, PIECE)
        return pltpu.make_async_remote_copy(
            src_ref=carried_own.at[rows],
            dst_ref=carried_in.at[rows],
            send_sem=shift_send.at[part],
            recv_sem=shift_recv.at[part],
            device_id={"segment": seg + 1},
        )

    def index_copy():
        return pltpu.make_async_remote_copy(
            src_ref=index_own,
            dst_ref=index_in,
            send_sem=shift_send.at[2],
            recv_sem=shift_recv.at[2],
            device_id={"segment": seg + 1},
        )

    def pair_copy(tick, number, kind):
        return pltpu.make_async_remote_copy(
            src_ref=pair_send.at[tick, number, kind],
            dst_ref=pair_recv.at[tick, number, kind],
            send_sem=pair_send_sem.at[tick, number, kind],
            recv_sem=pair_recv_sem.at[tick, number, kind],
            device_id={"tp": pair},
        )

    def far_copy(tick, number):
        return pltpu.make_async_remote_copy(
            src_ref=far_send.at[tick, number],
            dst_ref=far_recv.at[tick, number],
            send_sem=far_send_sem.at[tick, number],
            recv_sem=far_recv_sem.at[tick, number],
            device_id={"tp": far},
        )

    def out_copy(number):
        return pltpu.make_async_remote_copy(
            src_ref=first_out.at[number],
            dst_ref=out_in.at[number],
            send_sem=out_send_sem.at[number],
            recv_sem=out_recv_sem.at[number],
            device_id={"segment": seg + 1},
        )

    row_loads[0].wait()
    tokens[rows_of(0, core)] = normed(residual[...])
    row_loads[1].wait()
    carried_own[...] = (
        residual[...].astype(jnp.float32) + pending[...].astype(jnp.float32)
    ).astype(jnp.bfloat16)
    index_own[...] = jnp.full(index_own.shape, span_ref[0], jnp.int32)

    pl.semaphore_wait(barrier, 2 + has_prev.astype(jnp.int32) + has_next.astype(jnp.int32))

    for part in range(2):
        gather_copy(0, 0, part).start()

    @pl.when(has_next)
    def _():
        for part in range(2):
            shift_copy(part).start()
        index_copy().start()

    for part in range(2):
        gather_copy(0, 1, part).start()

    @pl.when(jnp.logical_not(has_prev))
    def _():
        carried_in[...] = jnp.zeros_like(carried_in)
        index_in[...] = jnp.zeros_like(index_in)
        out_in[...] = jnp.zeros_like(out_in)

    lane = lax.broadcasted_iota(jnp.int32, (SPAN, HD), 1)
    token = (lax.broadcasted_iota(jnp.int32, (SPAN, HD), 0) + side * HALF) & (SPAN - 1)
    key_token = (lane + side * HALF) & (SPAN - 1)

    def tables(tick, index_tile):
        positions = (index_tile[0:1, :] * SPAN + token).astype(jnp.float32)
        angles = positions * inverse_ref[0:1, :]
        sine = jnp.sin(angles)
        cosines[tick] = jnp.cos(angles)
        sines[tick] = jnp.where(lane < HD // 2, -sine, sine)

    def rotated(block, slot):
        tick, half = slot // 2, slot % 2
        rows = slice(half * HALF, (half + 1) * HALF)
        turned = pltpu.roll(block, HD // 2, 1)
        return (block * cosines[tick, rows] + turned * sines[tick, rows]).astype(jnp.bfloat16)

    causal_bias = jnp.where(key_token <= token, 0.0, MASKED).astype(jnp.float32)
    group = TILE // HALF
    slot_index = lax.broadcasted_iota(jnp.int32, (1, PREFIX), 1)
    slot_bias = jnp.where(slot_index < len_ref[0], 0.0, MASKED).astype(jnp.float32)
    score_scale = HD ** (-0.5) * math.log2(math.e)
    transposed = (((1,), (1,)), ((), ()))

    def relay_and_shift(part):
        gather_copy(0, 0, part).wait_recv()
        gather_copy(0, 2, part).start()

        @pl.when(has_prev)
        def _():
            shift_copy(part).wait_recv()

        rows = carried_in[part * PIECE : (part + 1) * PIECE]
        tokens[rows_of(2, core, part)] = normed(rows)
        gather_copy(1, 0, part).start()
        gather_copy(1, 1, part).start()

    def project(slots):
        first, count = slots[0] * HALF, len(slots) * HALF

        def tile(number, carry):
            columns = pl.ds(pl.multiple_of(number * WIDE, WIDE), WIDE)
            projected[:count, columns] = jnp.dot(
                tokens[first : first + count], w_query[:, columns], preferred_element_type=jnp.float32
            )
            return carry

        lax.fori_loop(0, query_width // WIDE, tile, 0)
        projected[:count, query_width:] = jnp.dot(
            tokens[first : first + count], w_kv[...], preferred_element_type=jnp.float32
        )

    def spread(slots):
        for place, slot in enumerate(slots):
            rows = slice(place * HALF, (place + 1) * HALF)
            for head in range(heads):
                block = projected[rows, head * HD : (head + 1) * HD]
                queries[slot, head * HALF : (head + 1) * HALF] = rotated(block, slot)
            tick, half = slot // 2, slot % 2
            span = slice(half * HALF, (half + 1) * HALF)
            fresh = projected[rows, query_width : query_width + HD].astype(jnp.bfloat16)
            span_keys[tick, span] = rotated(fresh.astype(jnp.float32), slot)
            span_values[tick, span] = projected[rows, query_width + HD :].astype(jnp.bfloat16)

    def attend_prefix(slot):
        half = slot % 2
        for block in range(heads // group):
            rows = slice(block * TILE, (block + 1) * TILE)
            scores = lax.dot_general(
                queries[slot, rows], keys[...], transposed, preferred_element_type=jnp.float32
            )
            scores = scores * score_scale + slot_bias
            peak = jnp.max(scores, axis=-1, keepdims=True)
            weights = jnp.exp2(scores - peak)
            total = jnp.sum(weights, axis=-1, keepdims=True)
            mixes[half, rows] = jnp.dot(
                weights.astype(jnp.bfloat16), values[...], preferred_element_type=jnp.float32
            )
            peaks[half, rows] = jnp.broadcast_to(peak, (TILE, HD))
            totals[half, rows] = jnp.broadcast_to(total, (TILE, HD))

    def attend_span(slot):
        tick, half = slot // 2, slot % 2
        bias = causal_bias[half * HALF : (half + 1) * HALF]
        bias = jnp.concatenate([bias] * group, 0)
        for block in range(heads // group):
            rows = slice(block * TILE, (block + 1) * TILE)
            scores = lax.dot_general(
                queries[slot, rows], span_keys[tick], transposed, preferred_element_type=jnp.float32
            )
            scores = scores * score_scale + bias
            before = peaks[half, rows]
            peak = jnp.maximum(before, jnp.max(scores, axis=-1, keepdims=True))
            weights = jnp.exp2(scores - peak)
            shrink = jnp.exp2(before - peak)
            total = totals[half, rows] * shrink + jnp.sum(weights, axis=-1, keepdims=True)
            mixed = mixes[half, rows] * shrink + jnp.dot(
                weights.astype(jnp.bfloat16), span_values[tick], preferred_element_type=jnp.float32
            )
            mixed = (mixed / total).astype(jnp.bfloat16)
            for place in range(group):
                head = block * group + place
                attended[half * HALF : (half + 1) * HALF, head * HD : (head + 1) * HD] = mixed[
                    place * HALF : (place + 1) * HALF
                ]

    def pass_on(tick, number):
        columns = slice(number * chunk, (number + 1) * chunk)
        pair_copy(tick, number, 1).wait_recv()
        far_send[tick, number] = (
            partial[rows_of(1, core), columns] + pair_recv[tick, number, 1].astype(jnp.float32)
        ).astype(jnp.bfloat16)
        far_copy(tick, number).start()

    def emit(tick, halves):
        first, last = halves[0] * HALF, (halves[-1] + 1) * HALF
        for number in range(OUT_CHUNKS):
            columns = slice(number * chunk, (number + 1) * chunk)
            partial[first:last, columns] = jnp.dot(
                attended[first:last], w_out[:, columns], preferred_element_type=jnp.float32
            )
            for kind in reversed(halves):
                pair_send[tick, number, kind] = partial[rows_of(kind, 1 - core), columns].astype(
                    jnp.bfloat16
                )
                pair_copy(tick, number, kind).start()
            if 1 in halves and number > 0:
                pass_on(tick, number - 1)
        if 1 in halves:
            pass_on(tick, OUT_CHUNKS - 1)

    def summed(tick, number):
        columns = slice(number * chunk, (number + 1) * chunk)
        pair_copy(tick, number, 0).wait_recv()
        beside = partial[rows_of(0, core), columns] + pair_recv[tick, number, 0].astype(jnp.float32)
        far_copy(tick, number).wait_recv()
        return (beside + far_recv[tick, number].astype(jnp.float32)).astype(jnp.bfloat16)

    def finish_first(number):
        first_out[number] = summed(0, number)

        @pl.when(has_next)
        def _():
            out_copy(number).start()

    tables(0, index_own[...])
    for part in range(2):
        gather_copy(0, 1, part).wait_recv()
    for load in loads[:5]:
        load.wait()
    project((0,))
    relay_and_shift(0)
    spread((0,))
    for load in loads[5:7]:
        load.wait()
    attend_prefix(0)
    relay_and_shift(1)

    @pl.when(has_prev)
    def _():
        index_copy().wait_recv()

    tables(1, index_in[...])
    for part in range(2):
        gather_copy(0, 2, part).wait_recv()
        gather_copy(1, 1, part).wait_recv()
    project((1, 2))
    spread((1, 2))
    attend_prefix(1)
    attend_span(1)
    attend_span(0)
    for load in loads[7:]:
        load.wait()
    for part in range(2):
        gather_copy(1, 0, part).wait_recv()
        gather_copy(1, 2, part).start()
    emit(0, (0, 1))

    for part in range(2):
        gather_copy(1, 2, part).wait_recv()
    project((3,))
    spread((3,))
    attend_prefix(3)
    attend_span(3)
    emit(1, (1,))
    for number in range(OUT_CHUNKS):
        finish_first(number)
    attend_prefix(2)
    attend_span(2)
    emit(1, (0,))
    for number in range(OUT_CHUNKS):
        columns = slice(number * chunk, (number + 1) * chunk)
        output_ref[0, :, columns] = summed(1, number)
    for number in range(OUT_CHUNKS):
        columns = slice(number * chunk, (number + 1) * chunk)

        @pl.when(has_prev)
        def _():
            out_copy(number).wait_recv()

        carried_ref[0, :, columns] = (
            carried_in[:, columns].astype(jnp.float32) + out_in[number].astype(jnp.float32)
        ).astype(jnp.bfloat16)

    for tick in range(2):
        for part in range(2):
            for leg in range(3):
                gather_copy(tick, leg, part).wait_send()
        for number in range(OUT_CHUNKS):
            for kind in range(2):
                pair_copy(tick, number, kind).wait_send()
            far_copy(tick, number).wait_send()

    @pl.when(has_next)
    def _():
        for part in range(2):
            shift_copy(part).wait_send()
        index_copy().wait_send()
        for number in range(OUT_CHUNKS):
            out_copy(number).wait_send()


def hand_out_kernel(carried_from, output_from, carried_to, output_to, sem):
    rows = carried_from.shape[1] // 2
    copies = [
        pltpu.make_async_copy(
            source.at[0, pl.ds(part * rows, rows)],
            target.at[0, pl.ds(part * rows, rows)],
            sem.at[place, part],
        )
        for place, (source, target) in enumerate(
            ((carried_from, carried_to), (output_from, output_to))
        )
        for part in range(2)
    ]
    for copy in copies:
        copy.start()
    for copy in copies:
        copy.wait()


def hand_out(carried, output):
    whole = pl.BlockSpec(memory_space=pl.ANY)
    shape = jax.ShapeDtypeStruct(carried.shape, carried.dtype)
    return pl.pallas_call(
        hand_out_kernel,
        out_shape=(shape, shape),
        in_specs=[whole, whole],
        out_specs=(whole, whole),
        scratch_shapes=[pltpu.SemaphoreType.DMA((2, 2))],
        compiler_params=pltpu.CompilerParams(vmem_limit_bytes=1024 * 1024),
        name="hand_out",
    )(carried, output)


def fused(
    sections,
    residual,
    pending,
    span_index,
    prefix_len,
    norm_gain,
    w_query,
    w_kv,
    w_out,
    prefix_cache,
):
    features, query_width = w_query.shape[1:]
    pair_width = w_kv.shape[2]
    chunk = features // OUT_CHUNKS
    exponents = -np.arange(0, HD, 2, dtype=np.float64) / HD
    inverse = np.tile((rope_base**exponents).astype(np.float32), 2)
    inverse = jnp.asarray(np.tile(inverse[None], (8, 1)))
    smem = pl.BlockSpec(memory_space=pltpu.SMEM)
    vmem = pl.BlockSpec(memory_space=pltpu.VMEM)
    whole = pl.BlockSpec(memory_space=pl.ANY)
    half = jnp.bfloat16
    dma = pltpu.SemaphoreType.DMA
    carried, output = pl.pallas_call(
        functools.partial(fused_kernel, sections),
        out_shape=(
            jax.ShapeDtypeStruct(residual.shape, half),
            jax.ShapeDtypeStruct(residual.shape, half),
        ),
        in_specs=[smem, smem, whole, whole, vmem, vmem, whole, whole, whole, whole],
        out_specs=(vmem, vmem),
        scratch_shapes=[
            pltpu.VMEM((ROWS, features), half),
            pltpu.VMEM((ROWS, features), half),
            pltpu.VMEM((features, query_width), half),
            pltpu.VMEM((features, pair_width), half),
            pltpu.VMEM((query_width, features), half),
            pltpu.VMEM((PREFIX, HD), half),
            pltpu.VMEM((PREFIX, HD), half),
            pltpu.VMEM((2, SPAN, HD), half),
            pltpu.VMEM((2, SPAN, HD), half),
            pltpu.VMEM((2 * SPAN, features), half),
            pltpu.VMEM((ROWS, features), half),
            pltpu.VMEM((ROWS, features), half),
            pltpu.VMEM((8, HD), jnp.int32),
            pltpu.VMEM((8, HD), jnp.int32),
            pltpu.VMEM((2, SPAN, HD), jnp.float32),
            pltpu.VMEM((2, SPAN, HD), jnp.float32),
            pltpu.VMEM((SPAN, query_width + pair_width), jnp.float32),
            pltpu.VMEM((4, query_width // HD * HALF, HD), half),
            pltpu.VMEM((2, query_width // HD * HALF, HD), jnp.float32),
            pltpu.VMEM((2, query_width // HD * HALF, HD), jnp.float32),
            pltpu.VMEM((2, query_width // HD * HALF, HD), jnp.float32),
            pltpu.VMEM((SPAN, query_width), half),
            pltpu.VMEM((SPAN, features), jnp.float32),
            pltpu.VMEM((2, OUT_CHUNKS, 2, ROWS, chunk), half),
            pltpu.VMEM((2, OUT_CHUNKS, 2, ROWS, chunk), half),
            pltpu.VMEM((2, OUT_CHUNKS, ROWS, chunk), half),
            pltpu.VMEM((2, OUT_CHUNKS, ROWS, chunk), half),
            pltpu.VMEM((OUT_CHUNKS, ROWS, chunk), half),
            pltpu.VMEM((OUT_CHUNKS, ROWS, chunk), half),
            dma((2,)),
            dma((11,)),
            dma((2, 3, 2)),
            dma((2, 3, 2)),
            dma((3,)),
            dma((3,)),
            dma((2, OUT_CHUNKS, 2)),
            dma((2, OUT_CHUNKS, 2)),
            dma((2, OUT_CHUNKS)),
            dma((2, OUT_CHUNKS)),
            dma((OUT_CHUNKS,)),
            dma((OUT_CHUNKS,)),
        ],
        compiler_params=pltpu.CompilerParams(
            collective_id=0, has_side_effects=True, vmem_limit_bytes=46 * 1024 * 1024
        ),
        name="fused_relay",
    )(
        span_index,
        prefix_len,
        residual,
        pending,
        norm_gain,
        inverse,
        w_query,
        w_kv,
        w_out,
        prefix_cache,
    )
    return hand_out(carried, output)


def solution(mesh):
    in_specs = (
        P("segment", "tp", None),
        P("segment", "tp", None),
        P("segment"),
        P("segment"),
        P("segment", None),
        P("segment", None, "tp"),
        P("segment", None, "tp"),
        P("segment", "tp", None),
        P("segment", "tp", None),
    )
    out_specs = (P("segment", "tp", None), P("segment", "tp", None))
    body = shards
    if mesh.shape["tp"] == TP == KV_HEADS and TICKS == 2:
        body = functools.partial(fused, mesh.shape["segment"])
    return jax.shard_map(body, mesh=mesh, in_specs=in_specs, out_specs=out_specs, check_vma=False)
```

```python
import functools
import math

import jax
import jax.numpy as jnp
import numpy as np
from jax import lax
from jax.experimental import pallas as pl
from jax.experimental.pallas import tpu as pltpu
from jax.sharding import PartitionSpec as P

KV_HEADS = 4
HD = 128
SPAN = 128
PREFIX = 1536
TICKS = 2


norm_eps = 1e-05
rope_base = 500000.0


def from_partner(array, axis, stride):
    return lax.ppermute(array, axis, [(i, i ^ 1 << stride) for i in range(lax.axis_size(axis))])


def shifted(block, axis, distance):
    devices = range(lax.axis_size(axis))
    route = [(i - distance, i) for i in devices if i - distance in devices]
    return lax.ppermute(block, axis, route)


def rotate(values, positions):
    half_width = values.shape[-1] // 2
    inverse = rope_base ** (
        -jnp.arange(0, values.shape[-1], 2, dtype=jnp.float32) / values.shape[-1]
    )
    angles = positions.astype(jnp.float32)[:, None] * inverse[None, :]
    cosine_table = jnp.cos(angles)[:, None, :]
    sine_table = jnp.sin(angles)[:, None, :]
    first_half = values[..., :half_width]
    second_half = values[..., half_width:]
    return jnp.concatenate(
        [
            first_half * cosine_table - second_half * sine_table,
            second_half * cosine_table + first_half * sine_table,
        ],
        axis=-1,
    )


def shards(
    residual, pending, span_index, prefix_len, norm_gain, w_query, w_kv, w_out, prefix_cache
):
    group_size = lax.axis_size("tp") // KV_HEADS
    group_bits = group_size.bit_length() - 1
    tp_place = lax.axis_index("tp")
    local_heads = w_query.shape[2] // HD
    weight_query = w_query[0]
    weight_pairs = w_kv[0]
    weight_out = w_out[0]
    query_width = weight_query.shape[1]
    gain_row = norm_gain[0].astype(jnp.float32)
    head_cache = prefix_cache[0]
    for bit_number in range(group_bits):
        partner = from_partner(head_cache, "tp", bit_number)
        lower_half = tp_place // (1 << bit_number) % 2 == 0
        head_cache = jnp.where(
            lower_half,
            jnp.concatenate([head_cache, partner], 0),
            jnp.concatenate([partner, head_cache], 0),
        )
    cache_keys = head_cache[:, :HD]
    cache_values = head_cache[:, HD:]
    slot_index = jnp.arange(PREFIX, dtype=jnp.int32)
    token_index = jnp.arange(SPAN, dtype=jnp.int32)
    causal = token_index[None, :] <= token_index[:, None]
    score_scale = HD ** (-0.5)
    rows_now = residual[0]
    pending_now = pending[0]
    index_now = span_index
    for segment_tick in range(TICKS):
        last_tick = segment_tick + 1 == TICKS
        widths = rows_now.astype(jnp.float32)
        mean_square = jnp.mean(widths * widths, axis=-1, keepdims=True)
        normed = (widths * lax.rsqrt(mean_square + norm_eps) * gain_row).astype(jnp.bfloat16)
        carried = (widths + pending_now.astype(jnp.float32)).astype(jnp.bfloat16)
        block_rows = lax.all_gather(normed, "tp", axis=0, tiled=True)
        projected = jnp.concatenate(
            [
                jnp.dot(block_rows, weight_query, preferred_element_type=jnp.float32),
                jnp.dot(block_rows, weight_pairs, preferred_element_type=jnp.float32),
            ],
            axis=1,
        )
        positions = index_now[0] * SPAN + token_index
        queries = rotate(
            projected[:, :query_width].reshape(SPAN, local_heads, HD), positions
        ).astype(jnp.bfloat16)
        fresh_head = projected[:, query_width:].astype(jnp.bfloat16)
        for bit_number in range(group_bits):
            partner = from_partner(fresh_head, "tp", bit_number)
            lower_half = tp_place // (1 << bit_number) % 2 == 0
            fresh_head = jnp.where(
                lower_half,
                jnp.concatenate([fresh_head, partner], 1),
                jnp.concatenate([partner, fresh_head], 1),
            )
        new_keys = rotate(fresh_head[:, None, :HD].astype(jnp.float32), positions)[:, 0, :].astype(
            jnp.bfloat16
        )
        new_values = fresh_head[:, HD:]
        score_prefix = (
            jnp.einsum("chd,pd->hcp", queries, cache_keys, preferred_element_type=jnp.float32)
            * score_scale
        )
        score_span = (
            jnp.einsum("chd,kd->hck", queries, new_keys, preferred_element_type=jnp.float32)
            * score_scale
        )
        score_prefix = jnp.where(
            (slot_index < prefix_len[0])[None, None, :], score_prefix, -jnp.inf
        )
        score_span = jnp.where(causal[None], score_span, -jnp.inf)
        row_peak = jnp.maximum(
            jnp.max(score_prefix, axis=-1, keepdims=True),
            jnp.max(score_span, axis=-1, keepdims=True),
        )
        exp_prefix = jnp.exp(score_prefix - row_peak)
        exp_span = jnp.exp(score_span - row_peak)
        denominator = jnp.sum(exp_prefix, axis=-1, keepdims=True) + jnp.sum(
            exp_span, axis=-1, keepdims=True
        )
        weight_prefix = (exp_prefix / denominator).astype(jnp.bfloat16)
        weight_span = (exp_span / denominator).astype(jnp.bfloat16)
        attended = jnp.einsum(
            "hcp,pd->chd", weight_prefix, cache_values, preferred_element_type=jnp.float32
        )
        attended = attended + jnp.einsum(
            "hck,kd->chd", weight_span, new_values, preferred_element_type=jnp.float32
        )
        attended = attended.astype(jnp.bfloat16).reshape(SPAN, local_heads * HD)
        summed = lax.psum_scatter(
            jnp.dot(attended, weight_out, preferred_element_type=jnp.float32),
            "tp",
            scatter_dimension=0,
            tiled=True,
        )
        output = summed.astype(jnp.bfloat16)
        if not last_tick:
            rows_now, pending_now, index_now = shifted((carried, output, index_now), "segment", 1)
    return (carried[None], output[None])


TP = 4
ROWS = SPAN // TP
HALF = 2 * ROWS
PIECE = ROWS // 2
OUT_CHUNKS = 4
TILE = 256
WIDE = 512
MASKED = -1e30


def fused_kernel(
    sections,
    span_ref,
    len_ref,
    residual_hbm,
    pending_hbm,
    gain_hbm,
    inverse_hbm,
    w_query_hbm,
    w_kv_hbm,
    w_out_hbm,
    cache_hbm,
    carried_ref,
    output_ref,
    residual,
    pending,
    gain_ref,
    inverse_ref,
    w_query,
    w_kv,
    w_out,
    keys,
    values,
    span_keys,
    span_values,
    tokens,
    carried_own,
    carried_in,
    index_own,
    index_in,
    cosines,
    sines,
    projected,
    queries,
    peaks,
    mixes,
    attended,
    partial,
    pair_send,
    pair_recv,
    far_send,
    far_recv,
    first_out,
    out_in,
    row_sem,
    load_sem,
    gather_send,
    gather_recv,
    shift_send,
    shift_recv,
    pair_send_sem,
    pair_recv_sem,
    far_send_sem,
    far_recv_sem,
    out_send_sem,
    out_recv_sem,
):
    features = w_query.shape[0]
    query_width = w_query.shape[1]
    heads = query_width // HD
    chunk = features // OUT_CHUNKS
    seg = lax.axis_index("segment")
    me = lax.axis_index("tp")
    core = lax.rem(me, 2)
    side = me // 2
    pair = me + 1 - 2 * core
    far = lax.rem(me + 2, TP)
    has_prev = seg > 0
    has_next = seg < sections - 1

    barrier = pltpu.get_barrier_semaphore()
    for partner in (pair, far):
        pl.semaphore_signal(barrier, inc=1, device_id={"tp": partner})

    @pl.when(has_prev)
    def _():
        pl.semaphore_signal(barrier, inc=1, device_id={"segment": seg - 1})

    @pl.when(has_next)
    def _():
        pl.semaphore_signal(barrier, inc=1, device_id={"segment": seg + 1})

    row_loads = [
        pltpu.make_async_copy(residual_hbm.at[0], residual, row_sem.at[0]),
        pltpu.make_async_copy(gain_hbm, gain_ref, row_sem.at[2]),
        pltpu.make_async_copy(pending_hbm.at[0], pending, row_sem.at[1]),
        pltpu.make_async_copy(inverse_hbm, inverse_ref, row_sem.at[3]),
    ]
    loads = []
    quarter = features // 4
    for part in range(4):
        span = pl.ds(part * quarter, quarter)
        loads.append((w_query_hbm.at[0, span], w_query.at[span]))
    loads.append((w_kv_hbm.at[0], w_kv))
    loads.append((cache_hbm.at[0, :, pl.ds(0, HD)], keys))
    loads.append((cache_hbm.at[0, :, pl.ds(HD, HD)], values.at[:, pl.ds(0, HD)]))
    quarter_out = query_width // 4
    for part in range(4):
        span = pl.ds(part * quarter_out, quarter_out)
        loads.append((w_out_hbm.at[0, span], w_out.at[span]))
    loads = [
        pltpu.make_async_copy(source, target, load_sem.at[number])
        for number, (source, target) in enumerate(loads)
    ]
    for load in row_loads + loads:
        load.start()

    def rows_of(slot, which, part=None):
        if part is None:
            return pl.ds(pl.multiple_of(slot * HALF + which * ROWS, ROWS), ROWS)
        return pl.ds(pl.multiple_of(slot * HALF + which * ROWS + part * PIECE, PIECE), PIECE)

    def normed(rows):
        widths = rows.astype(jnp.float32)
        gain = gain_ref[...].astype(jnp.float32)
        mean_square = jnp.mean(widths * widths, axis=-1, keepdims=True)
        return (widths * lax.rsqrt(mean_square + norm_eps) * gain).astype(jnp.bfloat16)

    def gather_copy(tick, leg, part):
        here, there = ((0, 1), (0, 0), (1, 1))[leg]
        return pltpu.make_async_remote_copy(
            src_ref=tokens.at[rows_of(2 * tick + here, core, part)],
            dst_ref=tokens.at[rows_of(2 * tick + there, core, part)],
            send_sem=gather_send.at[tick, leg, part],
            recv_sem=gather_recv.at[tick, leg, part],
            device_id={"tp": far if leg == 0 else pair},
        )

    def shift_copy(part):
        rows = pl.ds(part * PIECE, PIECE)
        return pltpu.make_async_remote_copy(
            src_ref=carried_own.at[rows],
            dst_ref=carried_in.at[rows],
            send_sem=shift_send.at[part],
            recv_sem=shift_recv.at[part],
            device_id={"segment": seg + 1},
        )

    def index_copy():
        return pltpu.make_async_remote_copy(
            src_ref=index_own,
            dst_ref=index_in,
            send_sem=shift_send.at[2],
            recv_sem=shift_recv.at[2],
            device_id={"segment": seg + 1},
        )

    def pair_copy(tick, number, kind):
        return pltpu.make_async_remote_copy(
            src_ref=pair_send.at[tick, number, kind],
            dst_ref=pair_recv.at[tick, number, kind],
            send_sem=pair_send_sem.at[tick, number, kind],
            recv_sem=pair_recv_sem.at[tick, number, kind],
            device_id={"tp": pair},
        )

    def far_copy(tick, number):
        return pltpu.make_async_remote_copy(
            src_ref=far_send.at[tick, number],
            dst_ref=far_recv.at[tick, number],
            send_sem=far_send_sem.at[tick, number],
            recv_sem=far_recv_sem.at[tick, number],
            device_id={"tp": far},
        )

    def out_copy(number):
        return pltpu.make_async_remote_copy(
            src_ref=first_out.at[number],
            dst_ref=out_in.at[number],
            send_sem=out_send_sem.at[number],
            recv_sem=out_recv_sem.at[number],
            device_id={"segment": seg + 1},
        )

    row_loads[0].wait()
    row_loads[1].wait()
    tokens[rows_of(0, core)] = normed(residual[...])
    row_loads[2].wait()
    carried_own[...] = (
        residual[...].astype(jnp.float32) + pending[...].astype(jnp.float32)
    ).astype(jnp.bfloat16)
    index_own[...] = jnp.full(index_own.shape, span_ref[0], jnp.int32)

    pl.semaphore_wait(barrier, 2 + has_prev.astype(jnp.int32) + has_next.astype(jnp.int32))

    for part in range(2):
        gather_copy(0, 0, part).start()

    @pl.when(has_next)
    def _():
        for part in range(2):
            shift_copy(part).start()
        index_copy().start()

    for part in range(2):
        gather_copy(0, 1, part).start()

    @pl.when(jnp.logical_not(has_prev))
    def _():
        carried_in[...] = jnp.zeros_like(carried_in)
        index_in[...] = jnp.zeros_like(index_in)
        out_in[...] = jnp.zeros_like(out_in)

    lane = lax.broadcasted_iota(jnp.int32, (SPAN, HD), 1)
    token = (lax.broadcasted_iota(jnp.int32, (SPAN, HD), 0) + side * HALF) & (SPAN - 1)
    key_token = (lane + side * HALF) & (SPAN - 1)

    def tables(tick, index_tile):
        positions = (index_tile[0:1, :] * SPAN + token).astype(jnp.float32)
        angles = positions * inverse_ref[0:1, :]
        sine = jnp.sin(angles)
        cosines[tick] = jnp.cos(angles)
        sines[tick] = jnp.where(lane < HD // 2, -sine, sine)

    def rotated(block, slot):
        tick, half = slot // 2, slot % 2
        rows = slice(half * HALF, (half + 1) * HALF)
        turned = pltpu.roll(block, HD // 2, 1)
        return (block * cosines[tick, rows] + turned * sines[tick, rows]).astype(jnp.bfloat16)

    causal_bias = jnp.where(key_token <= token, 0.0, MASKED).astype(jnp.float32)
    group = TILE // HALF
    slot_index = lax.broadcasted_iota(jnp.int32, (1, PREFIX), 1)
    slot_bias = jnp.where(slot_index < len_ref[0], 0.0, MASKED).astype(jnp.float32)
    score_scale = HD ** (-0.5) * math.log2(math.e)
    transposed = (((1,), (1,)), ((), ()))

    def relay_and_shift(part):
        gather_copy(0, 0, part).wait_recv()
        gather_copy(0, 2, part).start()

        @pl.when(has_prev)
        def _():
            shift_copy(part).wait_recv()

        rows = carried_in[part * PIECE : (part + 1) * PIECE]
        tokens[rows_of(2, core, part)] = normed(rows)
        gather_copy(1, 0, part).start()
        gather_copy(1, 1, part).start()

    def project(slots):
        first, count = slots[0] * HALF, len(slots) * HALF

        def tile(number, carry):
            columns = pl.ds(pl.multiple_of(number * WIDE, WIDE), WIDE)
            projected[:count, columns] = jnp.dot(
                tokens[first : first + count], w_query[:, columns], preferred_element_type=jnp.float32
            )
            return carry

        lax.fori_loop(0, query_width // WIDE, tile, 0)
        projected[:count, query_width:] = jnp.dot(
            tokens[first : first + count], w_kv[...], preferred_element_type=jnp.float32
        )

    def spread(slots):
        for place, slot in enumerate(slots):
            rows = slice(place * HALF, (place + 1) * HALF)
            for head in range(heads):
                block = projected[rows, head * HD : (head + 1) * HD]
                queries[slot, head * HALF : (head + 1) * HALF] = rotated(block, slot)
            tick, half = slot // 2, slot % 2
            span = slice(half * HALF, (half + 1) * HALF)
            fresh = projected[rows, query_width : query_width + HD].astype(jnp.bfloat16)
            span_keys[tick, span] = rotated(fresh.astype(jnp.float32), slot)
            span_values[tick, span, :HD] = projected[rows, query_width + HD :].astype(jnp.bfloat16)

    def attend_prefix(slot):
        half = slot % 2
        for block in range(heads // group):
            rows = slice(block * TILE, (block + 1) * TILE)
            scores = lax.dot_general(
                queries[slot, rows], keys[...], transposed, preferred_element_type=jnp.float32
            )
            scores = scores * score_scale + slot_bias
            peak = jnp.max(scores, axis=-1, keepdims=True)
            weights = jnp.exp2(scores - peak)
            mixes[half, rows] = jnp.dot(
                weights.astype(jnp.bfloat16), values[...], preferred_element_type=jnp.float32
            )
            peaks[half, rows] = jnp.broadcast_to(peak, (TILE, HD))

    def attend_span(slot):
        tick, half = slot // 2, slot % 2
        bias = causal_bias[half * HALF : (half + 1) * HALF]
        bias = jnp.concatenate([bias] * group, 0)
        for block in range(heads // group):
            rows = slice(block * TILE, (block + 1) * TILE)
            scores = lax.dot_general(
                queries[slot, rows], span_keys[tick], transposed, preferred_element_type=jnp.float32
            )
            scores = scores * score_scale + bias
            before = peaks[half, rows]
            peak = jnp.maximum(before, jnp.max(scores, axis=-1, keepdims=True))
            weights = jnp.exp2(scores - peak)
            shrink = jnp.exp2(before - peak)
            fresh = jnp.dot(
                weights.astype(jnp.bfloat16), span_values[tick], preferred_element_type=jnp.float32
            )
            total = mixes[half, rows, HD:] * shrink + fresh[:, HD:]
            mixed = mixes[half, rows, :HD] * shrink + fresh[:, :HD]
            mixed = (mixed / total).astype(jnp.bfloat16)
            for place in range(group):
                head = block * group + place
                attended[half * HALF : (half + 1) * HALF, head * HD : (head + 1) * HD] = mixed[
                    place * HALF : (place + 1) * HALF
                ]

    def pass_on(tick, number):
        columns = slice(number * chunk, (number + 1) * chunk)
        pair_copy(tick, number, 1).wait_recv()
        far_send[tick, number] = (
            partial[rows_of(1, core), columns] + pair_recv[tick, number, 1].astype(jnp.float32)
        ).astype(jnp.bfloat16)
        far_copy(tick, number).start()

    def emit(tick, halves):
        first, last = halves[0] * HALF, (halves[-1] + 1) * HALF
        for number in range(OUT_CHUNKS):
            columns = slice(number * chunk, (number + 1) * chunk)
            partial[first:last, columns] = jnp.dot(
                attended[first:last], w_out[:, columns], preferred_element_type=jnp.float32
            )
            for kind in reversed(halves):
                pair_send[tick, number, kind] = partial[rows_of(kind, 1 - core), columns].astype(
                    jnp.bfloat16
                )
                pair_copy(tick, number, kind).start()
        if 1 in halves:
            for number in range(OUT_CHUNKS):
                pass_on(tick, number)

    def summed(tick, number):
        columns = slice(number * chunk, (number + 1) * chunk)
        pair_copy(tick, number, 0).wait_recv()
        beside = partial[rows_of(0, core), columns] + pair_recv[tick, number, 0].astype(jnp.float32)
        far_copy(tick, number).wait_recv()
        return (beside + far_recv[tick, number].astype(jnp.float32)).astype(jnp.bfloat16)

    def finish_first(number):
        first_out[number] = summed(0, number)

        @pl.when(has_next)
        def _():
            out_copy(number).start()

    row_loads[3].wait()
    tables(0, index_own[...])
    values[:, HD:] = jnp.ones_like(values[:, HD:])
    span_values[:, :, HD:] = jnp.ones_like(span_values[:, :, HD:])
    for part in range(2):
        gather_copy(0, 1, part).wait_recv()
    for load in loads[:5]:
        load.wait()
    project((0,))
    relay_and_shift(0)
    spread((0,))
    for load in loads[5:7]:
        load.wait()
    attend_prefix(0)
    relay_and_shift(1)

    @pl.when(has_prev)
    def _():
        index_copy().wait_recv()

    tables(1, index_in[...])
    for part in range(2):
        gather_copy(0, 2, part).wait_recv()
        gather_copy(1, 1, part).wait_recv()
    project((1, 2))
    spread((1, 2))
    attend_prefix(1)
    attend_span(1)
    attend_span(0)
    for load in loads[7:]:
        load.wait()
    for part in range(2):
        gather_copy(1, 0, part).wait_recv()
        gather_copy(1, 2, part).start()
    emit(0, (0, 1))

    for part in range(2):
        gather_copy(1, 2, part).wait_recv()
    project((3,))
    spread((3,))
    attend_prefix(3)
    for number in range(OUT_CHUNKS // 2):
        finish_first(number)
    attend_span(3)
    emit(1, (1,))
    for number in range(OUT_CHUNKS // 2, OUT_CHUNKS):
        finish_first(number)
    attend_prefix(2)
    attend_span(2)
    emit(1, (0,))
    for number in range(OUT_CHUNKS):
        columns = slice(number * chunk, (number + 1) * chunk)
        output_ref[0, :, columns] = summed(1, number)
    for number in range(OUT_CHUNKS):
        columns = slice(number * chunk, (number + 1) * chunk)

        @pl.when(has_prev)
        def _():
            out_copy(number).wait_recv()

        carried_ref[0, :, columns] = (
            carried_in[:, columns].astype(jnp.float32) + out_in[number].astype(jnp.float32)
        ).astype(jnp.bfloat16)

    for tick in range(2):
        for part in range(2):
            for leg in range(3):
                gather_copy(tick, leg, part).wait_send()
        for number in range(OUT_CHUNKS):
            for kind in range(2):
                pair_copy(tick, number, kind).wait_send()
            far_copy(tick, number).wait_send()

    @pl.when(has_next)
    def _():
        for part in range(2):
            shift_copy(part).wait_send()
        index_copy().wait_send()
        for number in range(OUT_CHUNKS):
            out_copy(number).wait_send()


def hand_out_kernel(carried_from, output_from, carried_to, output_to, sem):
    rows = carried_from.shape[1] // 2
    copies = [
        pltpu.make_async_copy(
            source.at[0, pl.ds(part * rows, rows)],
            target.at[0, pl.ds(part * rows, rows)],
            sem.at[place, part],
        )
        for place, (source, target) in enumerate(
            ((carried_from, carried_to), (output_from, output_to))
        )
        for part in range(2)
    ]
    for copy in copies:
        copy.start()
    for copy in copies:
        copy.wait()


def hand_out(carried, output):
    whole = pl.BlockSpec(memory_space=pl.ANY)
    shape = jax.ShapeDtypeStruct(carried.shape, carried.dtype)
    return pl.pallas_call(
        hand_out_kernel,
        out_shape=(shape, shape),
        in_specs=[whole, whole],
        out_specs=(whole, whole),
        scratch_shapes=[pltpu.SemaphoreType.DMA((2, 2))],
        compiler_params=pltpu.CompilerParams(vmem_limit_bytes=60 * 1024 * 1024),
        name="hand_out",
    )(carried, output)


def fused(
    sections,
    residual,
    pending,
    span_index,
    prefix_len,
    norm_gain,
    w_query,
    w_kv,
    w_out,
    prefix_cache,
):
    features, query_width = w_query.shape[1:]
    pair_width = w_kv.shape[2]
    chunk = features // OUT_CHUNKS
    exponents = -np.arange(0, HD, 2, dtype=np.float64) / HD
    inverse = np.tile((rope_base**exponents).astype(np.float32), 2)
    inverse = jnp.asarray(np.tile(inverse[None], (8, 1)))
    smem = pl.BlockSpec(memory_space=pltpu.SMEM)
    vmem = pl.BlockSpec(memory_space=pltpu.VMEM)
    whole = pl.BlockSpec(memory_space=pltpu.HBM)
    half = jnp.bfloat16
    dma = pltpu.SemaphoreType.DMA
    carried, output = pl.pallas_call(
        functools.partial(fused_kernel, sections),
        out_shape=(
            jax.ShapeDtypeStruct(residual.shape, half),
            jax.ShapeDtypeStruct(residual.shape, half),
        ),
        in_specs=[smem, smem, whole, whole, whole, whole, whole, whole, whole, whole],
        out_specs=(vmem, vmem),
        scratch_shapes=[
            pltpu.VMEM((ROWS, features), half),
            pltpu.VMEM((ROWS, features), half),
            pltpu.VMEM((1, features), half),
            pltpu.VMEM((8, HD), jnp.float32),
            pltpu.VMEM((features, query_width), half),
            pltpu.VMEM((features, pair_width), half),
            pltpu.VMEM((query_width, features), half),
            pltpu.VMEM((PREFIX, HD), half),
            pltpu.VMEM((PREFIX, 2 * HD), half),
            pltpu.VMEM((2, SPAN, HD), half),
            pltpu.VMEM((2, SPAN, 2 * HD), half),
            pltpu.VMEM((2 * SPAN, features), half),
            pltpu.VMEM((ROWS, features), half),
            pltpu.VMEM((ROWS, features), half),
            pltpu.VMEM((8, HD), jnp.int32),
            pltpu.VMEM((8, HD), jnp.int32),
            pltpu.VMEM((2, SPAN, HD), jnp.float32),
            pltpu.VMEM((2, SPAN, HD), jnp.float32),
            pltpu.VMEM((SPAN, query_width + pair_width), jnp.float32),
            pltpu.VMEM((4, query_width // HD * HALF, HD), half),
            pltpu.VMEM((2, query_width // HD * HALF, HD), jnp.float32),
            pltpu.VMEM((2, query_width // HD * HALF, 2 * HD), jnp.float32),
            pltpu.VMEM((SPAN, query_width), half),
            pltpu.VMEM((SPAN, features), jnp.float32),
            pltpu.VMEM((2, OUT_CHUNKS, 2, ROWS, chunk), half),
            pltpu.VMEM((2, OUT_CHUNKS, 2, ROWS, chunk), half),
            pltpu.VMEM((2, OUT_CHUNKS, ROWS, chunk), half),
            pltpu.VMEM((2, OUT_CHUNKS, ROWS, chunk), half),
            pltpu.VMEM((OUT_CHUNKS, ROWS, chunk), half),
            pltpu.VMEM((OUT_CHUNKS, ROWS, chunk), half),
            dma((4,)),
            dma((11,)),
            dma((2, 3, 2)),
            dma((2, 3, 2)),
            dma((3,)),
            dma((3,)),
            dma((2, OUT_CHUNKS, 2)),
            dma((2, OUT_CHUNKS, 2)),
            dma((2, OUT_CHUNKS)),
            dma((2, OUT_CHUNKS)),
            dma((OUT_CHUNKS,)),
            dma((OUT_CHUNKS,)),
        ],
        compiler_params=pltpu.CompilerParams(
            collective_id=0, has_side_effects=True, vmem_limit_bytes=60 * 1024 * 1024
        ),
        name="fused_relay",
    )(
        span_index,
        prefix_len,
        residual,
        pending,
        norm_gain,
        inverse,
        w_query,
        w_kv,
        w_out,
        prefix_cache,
    )
    return hand_out(carried, output)


def solution(mesh):
    in_specs = (
        P("segment", "tp", None),
        P("segment", "tp", None),
        P("segment"),
        P("segment"),
        P("segment", None),
        P("segment", None, "tp"),
        P("segment", None, "tp"),
        P("segment", "tp", None),
        P("segment", "tp", None),
    )
    out_specs = (P("segment", "tp", None), P("segment", "tp", None))
    body = shards
    if mesh.shape["tp"] == TP == KV_HEADS and TICKS == 2:
        body = functools.partial(fused, mesh.shape["segment"])
    return jax.shard_map(body, mesh=mesh, in_specs=in_specs, out_specs=out_specs, check_vma=False)
```

```python
import functools
import math

import jax
import jax.numpy as jnp
import numpy as np
from jax import lax
from jax.experimental import pallas as pl
from jax.experimental.pallas import tpu as pltpu
from jax.sharding import PartitionSpec as P

KV_HEADS = 4
HD = 128
SPAN = 128
PREFIX = 1536
TICKS = 2


norm_eps = 1e-05
rope_base = 500000.0


def from_partner(array, axis, stride):
    return lax.ppermute(array, axis, [(i, i ^ 1 << stride) for i in range(lax.axis_size(axis))])


def shifted(block, axis, distance):
    devices = range(lax.axis_size(axis))
    route = [(i - distance, i) for i in devices if i - distance in devices]
    return lax.ppermute(block, axis, route)


def rotate(values, positions):
    half_width = values.shape[-1] // 2
    inverse = rope_base ** (
        -jnp.arange(0, values.shape[-1], 2, dtype=jnp.float32) / values.shape[-1]
    )
    angles = positions.astype(jnp.float32)[:, None] * inverse[None, :]
    cosine_table = jnp.cos(angles)[:, None, :]
    sine_table = jnp.sin(angles)[:, None, :]
    first_half = values[..., :half_width]
    second_half = values[..., half_width:]
    return jnp.concatenate(
        [
            first_half * cosine_table - second_half * sine_table,
            second_half * cosine_table + first_half * sine_table,
        ],
        axis=-1,
    )


def shards(
    residual, pending, span_index, prefix_len, norm_gain, w_query, w_kv, w_out, prefix_cache
):
    group_size = lax.axis_size("tp") // KV_HEADS
    group_bits = group_size.bit_length() - 1
    tp_place = lax.axis_index("tp")
    local_heads = w_query.shape[2] // HD
    weight_query = w_query[0]
    weight_pairs = w_kv[0]
    weight_out = w_out[0]
    query_width = weight_query.shape[1]
    gain_row = norm_gain[0].astype(jnp.float32)
    head_cache = prefix_cache[0]
    for bit_number in range(group_bits):
        partner = from_partner(head_cache, "tp", bit_number)
        lower_half = tp_place // (1 << bit_number) % 2 == 0
        head_cache = jnp.where(
            lower_half,
            jnp.concatenate([head_cache, partner], 0),
            jnp.concatenate([partner, head_cache], 0),
        )
    cache_keys = head_cache[:, :HD]
    cache_values = head_cache[:, HD:]
    slot_index = jnp.arange(PREFIX, dtype=jnp.int32)
    token_index = jnp.arange(SPAN, dtype=jnp.int32)
    causal = token_index[None, :] <= token_index[:, None]
    score_scale = HD ** (-0.5)
    rows_now = residual[0]
    pending_now = pending[0]
    index_now = span_index
    for segment_tick in range(TICKS):
        last_tick = segment_tick + 1 == TICKS
        widths = rows_now.astype(jnp.float32)
        mean_square = jnp.mean(widths * widths, axis=-1, keepdims=True)
        normed = (widths * lax.rsqrt(mean_square + norm_eps) * gain_row).astype(jnp.bfloat16)
        carried = (widths + pending_now.astype(jnp.float32)).astype(jnp.bfloat16)
        block_rows = lax.all_gather(normed, "tp", axis=0, tiled=True)
        projected = jnp.concatenate(
            [
                jnp.dot(block_rows, weight_query, preferred_element_type=jnp.float32),
                jnp.dot(block_rows, weight_pairs, preferred_element_type=jnp.float32),
            ],
            axis=1,
        )
        positions = index_now[0] * SPAN + token_index
        queries = rotate(
            projected[:, :query_width].reshape(SPAN, local_heads, HD), positions
        ).astype(jnp.bfloat16)
        fresh_head = projected[:, query_width:].astype(jnp.bfloat16)
        for bit_number in range(group_bits):
            partner = from_partner(fresh_head, "tp", bit_number)
            lower_half = tp_place // (1 << bit_number) % 2 == 0
            fresh_head = jnp.where(
                lower_half,
                jnp.concatenate([fresh_head, partner], 1),
                jnp.concatenate([partner, fresh_head], 1),
            )
        new_keys = rotate(fresh_head[:, None, :HD].astype(jnp.float32), positions)[:, 0, :].astype(
            jnp.bfloat16
        )
        new_values = fresh_head[:, HD:]
        score_prefix = (
            jnp.einsum("chd,pd->hcp", queries, cache_keys, preferred_element_type=jnp.float32)
            * score_scale
        )
        score_span = (
            jnp.einsum("chd,kd->hck", queries, new_keys, preferred_element_type=jnp.float32)
            * score_scale
        )
        score_prefix = jnp.where(
            (slot_index < prefix_len[0])[None, None, :], score_prefix, -jnp.inf
        )
        score_span = jnp.where(causal[None], score_span, -jnp.inf)
        row_peak = jnp.maximum(
            jnp.max(score_prefix, axis=-1, keepdims=True),
            jnp.max(score_span, axis=-1, keepdims=True),
        )
        exp_prefix = jnp.exp(score_prefix - row_peak)
        exp_span = jnp.exp(score_span - row_peak)
        denominator = jnp.sum(exp_prefix, axis=-1, keepdims=True) + jnp.sum(
            exp_span, axis=-1, keepdims=True
        )
        weight_prefix = (exp_prefix / denominator).astype(jnp.bfloat16)
        weight_span = (exp_span / denominator).astype(jnp.bfloat16)
        attended = jnp.einsum(
            "hcp,pd->chd", weight_prefix, cache_values, preferred_element_type=jnp.float32
        )
        attended = attended + jnp.einsum(
            "hck,kd->chd", weight_span, new_values, preferred_element_type=jnp.float32
        )
        attended = attended.astype(jnp.bfloat16).reshape(SPAN, local_heads * HD)
        summed = lax.psum_scatter(
            jnp.dot(attended, weight_out, preferred_element_type=jnp.float32),
            "tp",
            scatter_dimension=0,
            tiled=True,
        )
        output = summed.astype(jnp.bfloat16)
        if not last_tick:
            rows_now, pending_now, index_now = shifted((carried, output, index_now), "segment", 1)
    return (carried[None], output[None])


TP = 4
ROWS = SPAN // TP
HALF = 2 * ROWS
PIECE = ROWS // 2
OUT_CHUNKS = 4
TILE = 256
WIDE = 512
MASKED = -1e30


def fused_kernel(
    sections,
    span_ref,
    len_ref,
    residual_hbm,
    pending_hbm,
    gain_hbm,
    w_query_hbm,
    w_kv_hbm,
    w_out_hbm,
    cache_hbm,
    carried_ref,
    output_ref,
    residual,
    pending,
    gain_ref,
    w_query,
    w_kv,
    w_out,
    keys,
    values,
    span_keys,
    span_values,
    tokens,
    carried_own,
    carried_in,
    index_own,
    index_in,
    cosines,
    sines,
    projected,
    queries,
    peaks,
    totals,
    mixes,
    attended,
    partial,
    pair_send,
    pair_recv,
    far_send,
    far_recv,
    first_out,
    out_in,
    row_sem,
    load_sem,
    gather_send,
    gather_recv,
    shift_send,
    shift_recv,
    pair_send_sem,
    pair_recv_sem,
    far_send_sem,
    far_recv_sem,
    out_send_sem,
    out_recv_sem,
):
    features = w_query.shape[0]
    query_width = w_query.shape[1]
    heads = query_width // HD
    chunk = features // OUT_CHUNKS
    seg = lax.axis_index("segment")
    me = lax.axis_index("tp")
    core = lax.rem(me, 2)
    side = me // 2
    pair = me + 1 - 2 * core
    far = lax.rem(me + 2, TP)
    has_prev = seg > 0
    has_next = seg < sections - 1

    barrier = pltpu.get_barrier_semaphore()
    for partner in (pair, far):
        pl.semaphore_signal(barrier, inc=1, device_id={"tp": partner})

    @pl.when(has_prev)
    def _():
        pl.semaphore_signal(barrier, inc=1, device_id={"segment": seg - 1})

    @pl.when(has_next)
    def _():
        pl.semaphore_signal(barrier, inc=1, device_id={"segment": seg + 1})

    row_loads = [
        pltpu.make_async_copy(residual_hbm.at[0], residual, row_sem.at[0]),
        pltpu.make_async_copy(gain_hbm, gain_ref, row_sem.at[2]),
        pltpu.make_async_copy(pending_hbm.at[0], pending, row_sem.at[1]),
    ]
    loads = []
    quarter = features // 4
    for part in range(4):
        span = pl.ds(part * quarter, quarter)
        loads.append((w_query_hbm.at[0, span], w_query.at[span]))
    loads.append((w_kv_hbm.at[0], w_kv))
    loads.append((cache_hbm.at[0, :, pl.ds(0, HD)], keys))
    loads.append((cache_hbm.at[0, :, pl.ds(HD, HD)], values))
    quarter_out = query_width // 4
    for part in range(4):
        span = pl.ds(part * quarter_out, quarter_out)
        loads.append((w_out_hbm.at[0, span], w_out.at[span]))
    loads = [
        pltpu.make_async_copy(source, target, load_sem.at[number])
        for number, (source, target) in enumerate(loads)
    ]
    for load in row_loads:
        load.start()

    def rows_of(slot, which, part=None):
        if part is None:
            return pl.ds(pl.multiple_of(slot * HALF + which * ROWS, ROWS), ROWS)
        return pl.ds(pl.multiple_of(slot * HALF + which * ROWS + part * PIECE, PIECE), PIECE)

    def normed(rows):
        widths = rows.astype(jnp.float32)
        gain = gain_ref[...].astype(jnp.float32)
        mean_square = jnp.mean(widths * widths, axis=-1, keepdims=True)
        return (widths * lax.rsqrt(mean_square + norm_eps) * gain).astype(jnp.bfloat16)

    def gather_copy(tick, leg, part):
        here, there = ((0, 1), (0, 0), (1, 1))[leg]
        return pltpu.make_async_remote_copy(
            src_ref=tokens.at[rows_of(2 * tick + here, core, part)],
            dst_ref=tokens.at[rows_of(2 * tick + there, core, part)],
            send_sem=gather_send.at[tick, leg, part],
            recv_sem=gather_recv.at[tick, leg, part],
            device_id={"tp": far if leg == 0 else pair},
        )

    def shift_copy(part):
        rows = pl.ds(part * PIECE, PIECE)
        return pltpu.make_async_remote_copy(
            src_ref=carried_own.at[rows],
            dst_ref=carried_in.at[rows],
            send_sem=shift_send.at[part],
            recv_sem=shift_recv.at[part],
            device_id={"segment": seg + 1},
        )

    def index_copy():
        return pltpu.make_async_remote_copy(
            src_ref=index_own,
            dst_ref=index_in,
            send_sem=shift_send.at[2],
            recv_sem=shift_recv.at[2],
            device_id={"segment": seg + 1},
        )

    def pair_copy(tick, number, kind):
        return pltpu.make_async_remote_copy(
            src_ref=pair_send.at[tick, number, kind],
            dst_ref=pair_recv.at[tick, number, kind],
            send_sem=pair_send_sem.at[tick, number, kind],
            recv_sem=pair_recv_sem.at[tick, number, kind],
            device_id={"tp": pair},
        )

    def far_copy(tick, number):
        return pltpu.make_async_remote_copy(
            src_ref=far_send.at[tick, number],
            dst_ref=far_recv.at[tick, number],
            send_sem=far_send_sem.at[tick, number],
            recv_sem=far_recv_sem.at[tick, number],
            device_id={"tp": far},
        )

    def out_copy(number):
        return pltpu.make_async_remote_copy(
            src_ref=first_out.at[number],
            dst_ref=out_in.at[number],
            send_sem=out_send_sem.at[number],
            recv_sem=out_recv_sem.at[number],
            device_id={"segment": seg + 1},
        )

    row_loads[0].wait()
    row_loads[1].wait()
    for load in loads:
        load.start()
    tokens[rows_of(0, core)] = normed(residual[...])
    row_loads[2].wait()
    carried_own[...] = (
        residual[...].astype(jnp.float32) + pending[...].astype(jnp.float32)
    ).astype(jnp.bfloat16)
    index_own[...] = jnp.full(index_own.shape, span_ref[0], jnp.int32)

    pl.semaphore_wait(barrier, 2 + has_prev.astype(jnp.int32) + has_next.astype(jnp.int32))

    for part in range(2):
        gather_copy(0, 0, part).start()

    @pl.when(has_next)
    def _():
        for part in range(2):
            shift_copy(part).start()
        index_copy().start()

    for part in range(2):
        gather_copy(0, 1, part).start()

    @pl.when(jnp.logical_not(has_prev))
    def _():
        carried_in[...] = jnp.zeros_like(carried_in)
        index_in[...] = jnp.zeros_like(index_in)
        out_in[...] = jnp.zeros_like(out_in)

    lane = lax.broadcasted_iota(jnp.int32, (SPAN, HD), 1)
    token = (lax.broadcasted_iota(jnp.int32, (SPAN, HD), 0) + side * HALF) & (SPAN - 1)
    inverse = jnp.zeros((1, HD), jnp.float32)
    frequencies = (rope_base ** (-np.arange(0, HD, 2, dtype=np.float64) / HD)).astype(np.float32)
    for place, frequency in enumerate(frequencies):
        inverse = jnp.where(lane[0:1] % (HD // 2) == place, float(frequency), inverse)
    key_token = (lane + side * HALF) & (SPAN - 1)

    def tables(tick, index_tile):
        positions = (index_tile[0:1, :] * SPAN + token).astype(jnp.float32)
        angles = positions * inverse
        sine = jnp.sin(angles)
        cosines[tick] = jnp.cos(angles)
        sines[tick] = jnp.where(lane < HD // 2, -sine, sine)

    def rotated(block, slot):
        tick, half = slot // 2, slot % 2
        rows = slice(half * HALF, (half + 1) * HALF)
        turned = pltpu.roll(block, HD // 2, 1)
        return (block * cosines[tick, rows] + turned * sines[tick, rows]).astype(jnp.bfloat16)

    causal_bias = jnp.where(key_token <= token, 0.0, MASKED).astype(jnp.float32)
    group = TILE // HALF
    slot_index = lax.broadcasted_iota(jnp.int32, (1, PREFIX), 1)
    slot_bias = jnp.where(slot_index < len_ref[0], 0.0, MASKED).astype(jnp.float32)
    score_scale = HD ** (-0.5) * math.log2(math.e)
    transposed = (((1,), (1,)), ((), ()))

    def relay_and_shift(part):
        gather_copy(0, 0, part).wait_recv()
        gather_copy(0, 2, part).start()

        @pl.when(has_prev)
        def _():
            shift_copy(part).wait_recv()

        rows = carried_in[part * PIECE : (part + 1) * PIECE]
        tokens[rows_of(2, core, part)] = normed(rows)
        gather_copy(1, 0, part).start()
        gather_copy(1, 1, part).start()

    def project(slots):
        first, count = slots[0] * HALF, len(slots) * HALF

        def tile(number, carry):
            columns = pl.ds(pl.multiple_of(number * WIDE, WIDE), WIDE)
            projected[:count, columns] = jnp.dot(
                tokens[first : first + count], w_query[:, columns], preferred_element_type=jnp.float32
            )
            return carry

        lax.fori_loop(0, query_width // WIDE, tile, 0)
        projected[:count, query_width:] = jnp.dot(
            tokens[first : first + count], w_kv[...], preferred_element_type=jnp.float32
        )

    def spread(slots):
        for place, slot in enumerate(slots):
            rows = slice(place * HALF, (place + 1) * HALF)
            for head in range(heads):
                block = projected[rows, head * HD : (head + 1) * HD]
                queries[slot, head * HALF : (head + 1) * HALF] = rotated(block, slot)
            tick, half = slot // 2, slot % 2
            span = slice(half * HALF, (half + 1) * HALF)
            fresh = projected[rows, query_width : query_width + HD].astype(jnp.bfloat16)
            span_keys[tick, span] = rotated(fresh.astype(jnp.float32), slot)
            span_values[tick, span] = projected[rows, query_width + HD :].astype(jnp.bfloat16)

    def attend_prefix(slot):
        half = slot % 2
        for block in range(heads // group):
            rows = slice(block * TILE, (block + 1) * TILE)
            scores = lax.dot_general(
                queries[slot, rows], keys[...], transposed, preferred_element_type=jnp.float32
            )
            scores = scores * score_scale + slot_bias
            peak = jnp.max(scores, axis=-1, keepdims=True)
            weights = jnp.exp2(scores - peak)
            total = jnp.sum(weights, axis=-1, keepdims=True)
            mixes[half, rows] = jnp.dot(
                weights.astype(jnp.bfloat16), values[...], preferred_element_type=jnp.float32
            )
            peaks[half, rows] = jnp.broadcast_to(peak, (TILE, HD))
            totals[half, rows] = jnp.broadcast_to(total, (TILE, HD))

    def attend_span(slot):
        tick, half = slot // 2, slot % 2
        bias = causal_bias[half * HALF : (half + 1) * HALF]
        bias = jnp.concatenate([bias] * group, 0)
        for block in range(heads // group):
            rows = slice(block * TILE, (block + 1) * TILE)
            scores = lax.dot_general(
                queries[slot, rows], span_keys[tick], transposed, preferred_element_type=jnp.float32
            )
            scores = scores * score_scale + bias
            before = peaks[half, rows]
            peak = jnp.maximum(before, jnp.max(scores, axis=-1, keepdims=True))
            weights = jnp.exp2(scores - peak)
            shrink = jnp.exp2(before - peak)
            fresh = jnp.dot(
                weights.astype(jnp.bfloat16), span_values[tick], preferred_element_type=jnp.float32
            )
            total = totals[half, rows] * shrink + jnp.sum(weights, axis=-1, keepdims=True)
            mixed = mixes[half, rows] * shrink + fresh
            mixed = (mixed / total).astype(jnp.bfloat16)
            for place in range(group):
                head = block * group + place
                attended[half * HALF : (half + 1) * HALF, head * HD : (head + 1) * HD] = mixed[
                    place * HALF : (place + 1) * HALF
                ]

    def pass_on(tick, number):
        columns = slice(number * chunk, (number + 1) * chunk)
        pair_copy(tick, number, 1).wait_recv()
        far_send[tick, number] = (
            partial[rows_of(1, core), columns] + pair_recv[tick, number, 1].astype(jnp.float32)
        ).astype(jnp.bfloat16)
        far_copy(tick, number).start()

    def emit(tick, halves):
        first, last = halves[0] * HALF, (halves[-1] + 1) * HALF
        for number in range(OUT_CHUNKS):
            columns = slice(number * chunk, (number + 1) * chunk)
            partial[first:last, columns] = jnp.dot(
                attended[first:last], w_out[:, columns], preferred_element_type=jnp.float32
            )
            for kind in reversed(halves):
                pair_send[tick, number, kind] = partial[rows_of(kind, 1 - core), columns].astype(
                    jnp.bfloat16
                )
                pair_copy(tick, number, kind).start()
            if 1 in halves and number > 1:
                pass_on(tick, number - 2)
        if 1 in halves:
            for number in range(OUT_CHUNKS - 2, OUT_CHUNKS):
                pass_on(tick, number)

    def summed(tick, number):
        columns = slice(number * chunk, (number + 1) * chunk)
        pair_copy(tick, number, 0).wait_recv()
        beside = partial[rows_of(0, core), columns] + pair_recv[tick, number, 0].astype(jnp.float32)
        far_copy(tick, number).wait_recv()
        return (beside + far_recv[tick, number].astype(jnp.float32)).astype(jnp.bfloat16)

    def finish_first(number):
        first_out[number] = summed(0, number)

        @pl.when(has_next)
        def _():
            out_copy(number).start()

    tables(0, index_own[...])
    for part in range(2):
        gather_copy(0, 1, part).wait_recv()
    for load in loads[:5]:
        load.wait()
    project((0,))
    relay_and_shift(0)
    spread((0,))
    for load in loads[5:7]:
        load.wait()
    attend_prefix(0)
    relay_and_shift(1)

    @pl.when(has_prev)
    def _():
        index_copy().wait_recv()

    tables(1, index_in[...])
    for part in range(2):
        gather_copy(0, 2, part).wait_recv()
        gather_copy(1, 1, part).wait_recv()
    project((1, 2))
    spread((1, 2))
    attend_prefix(1)
    attend_span(1)
    attend_span(0)
    for load in loads[7:]:
        load.wait()
    for part in range(2):
        gather_copy(1, 0, part).wait_recv()
        gather_copy(1, 2, part).start()
    emit(0, (0, 1))

    for part in range(2):
        gather_copy(1, 2, part).wait_recv()
    project((3,))
    spread((3,))
    attend_prefix(3)
    attend_span(3)
    for number in range(OUT_CHUNKS // 2):
        finish_first(number)
    emit(1, (1,))
    for number in range(OUT_CHUNKS // 2, OUT_CHUNKS):
        finish_first(number)
    attend_prefix(2)
    attend_span(2)
    emit(1, (0,))
    for number in range(OUT_CHUNKS):
        columns = slice(number * chunk, (number + 1) * chunk)
        output_ref[0, :, columns] = summed(1, number)
    for number in range(OUT_CHUNKS):
        columns = slice(number * chunk, (number + 1) * chunk)

        @pl.when(has_prev)
        def _():
            out_copy(number).wait_recv()

        carried_ref[0, :, columns] = (
            carried_in[:, columns].astype(jnp.float32) + out_in[number].astype(jnp.float32)
        ).astype(jnp.bfloat16)

    for tick in range(2):
        for part in range(2):
            for leg in range(3):
                gather_copy(tick, leg, part).wait_send()
        for number in range(OUT_CHUNKS):
            for kind in range(2):
                pair_copy(tick, number, kind).wait_send()
            far_copy(tick, number).wait_send()

    @pl.when(has_next)
    def _():
        for part in range(2):
            shift_copy(part).wait_send()
        index_copy().wait_send()
        for number in range(OUT_CHUNKS):
            out_copy(number).wait_send()


def hand_out_kernel(carried_from, output_from, carried_to, output_to, sem):
    rows = carried_from.shape[1] // 2
    copies = [
        pltpu.make_async_copy(
            source.at[0, pl.ds(part * rows, rows)],
            target.at[0, pl.ds(part * rows, rows)],
            sem.at[place, part],
        )
        for place, (source, target) in enumerate(
            ((carried_from, carried_to), (output_from, output_to))
        )
        for part in range(2)
    ]
    for copy in copies:
        copy.start()
    for copy in copies:
        copy.wait()


def hand_out(carried, output):
    near = pl.BlockSpec(memory_space=pltpu.VMEM)
    whole = pl.BlockSpec(memory_space=pl.ANY)
    shape = jax.ShapeDtypeStruct(carried.shape, carried.dtype)
    return pl.pallas_call(
        hand_out_kernel,
        out_shape=(shape, shape),
        in_specs=[near, near],
        out_specs=(whole, whole),
        scratch_shapes=[pltpu.SemaphoreType.DMA((2, 2))],
        compiler_params=pltpu.CompilerParams(vmem_limit_bytes=4 * 1024 * 1024),
        name="hand_out",
    )(carried, output)


def fused(
    sections,
    residual,
    pending,
    span_index,
    prefix_len,
    norm_gain,
    w_query,
    w_kv,
    w_out,
    prefix_cache,
):
    features, query_width = w_query.shape[1:]
    pair_width = w_kv.shape[2]
    chunk = features // OUT_CHUNKS
    smem = pl.BlockSpec(memory_space=pltpu.SMEM)
    vmem = pl.BlockSpec(memory_space=pltpu.VMEM)
    whole = pl.BlockSpec(memory_space=pl.ANY)
    half = jnp.bfloat16
    dma = pltpu.SemaphoreType.DMA
    carried, output = pl.pallas_call(
        functools.partial(fused_kernel, sections),
        out_shape=(
            jax.ShapeDtypeStruct(residual.shape, half),
            jax.ShapeDtypeStruct(residual.shape, half),
        ),
        in_specs=[smem, smem] + [whole] * 7,
        out_specs=(vmem, vmem),
        scratch_shapes=[
            pltpu.VMEM((ROWS, features), half),
            pltpu.VMEM((ROWS, features), half),
            pltpu.VMEM((1, features), half),
            pltpu.VMEM((features, query_width), half),
            pltpu.VMEM((features, pair_width), half),
            pltpu.VMEM((query_width, features), half),
            pltpu.VMEM((PREFIX, HD), half),
            pltpu.VMEM((PREFIX, HD), half),
            pltpu.VMEM((2, SPAN, HD), half),
            pltpu.VMEM((2, SPAN, HD), half),
            pltpu.VMEM((2 * SPAN, features), half),
            pltpu.VMEM((ROWS, features), half),
            pltpu.VMEM((ROWS, features), half),
            pltpu.VMEM((8, HD), jnp.int32),
            pltpu.VMEM((8, HD), jnp.int32),
            pltpu.VMEM((2, SPAN, HD), jnp.float32),
            pltpu.VMEM((2, SPAN, HD), jnp.float32),
            pltpu.VMEM((SPAN, query_width + pair_width), jnp.float32),
            pltpu.VMEM((4, query_width // HD * HALF, HD), half),
            pltpu.VMEM((2, query_width // HD * HALF, HD), jnp.float32),
            pltpu.VMEM((2, query_width // HD * HALF, HD), jnp.float32),
            pltpu.VMEM((2, query_width // HD * HALF, HD), jnp.float32),
            pltpu.VMEM((SPAN, query_width), half),
            pltpu.VMEM((SPAN, features), jnp.float32),
            pltpu.VMEM((2, OUT_CHUNKS, 2, ROWS, chunk), half),
            pltpu.VMEM((2, OUT_CHUNKS, 2, ROWS, chunk), half),
            pltpu.VMEM((2, OUT_CHUNKS, ROWS, chunk), half),
            pltpu.VMEM((2, OUT_CHUNKS, ROWS, chunk), half),
            pltpu.VMEM((OUT_CHUNKS, ROWS, chunk), half),
            pltpu.VMEM((OUT_CHUNKS, ROWS, chunk), half),
            dma((3,)),
            dma((11,)),
            dma((2, 3, 2)),
            dma((2, 3, 2)),
            dma((3,)),
            dma((3,)),
            dma((2, OUT_CHUNKS, 2)),
            dma((2, OUT_CHUNKS, 2)),
            dma((2, OUT_CHUNKS)),
            dma((2, OUT_CHUNKS)),
            dma((OUT_CHUNKS,)),
            dma((OUT_CHUNKS,)),
        ],
        compiler_params=pltpu.CompilerParams(
            collective_id=0, has_side_effects=True, vmem_limit_bytes=54528 * 1024
        ),
        name="fused_relay",
    )(
        span_index,
        prefix_len,
        residual,
        pending,
        norm_gain,
        w_query,
        w_kv,
        w_out,
        prefix_cache,
    )
    return hand_out(carried, output)


def solution(mesh):
    in_specs = (
        P("segment", "tp", None),
        P("segment", "tp", None),
        P("segment"),
        P("segment"),
        P("segment", None),
        P("segment", None, "tp"),
        P("segment", None, "tp"),
        P("segment", "tp", None),
        P("segment", "tp", None),
    )
    out_specs = (P("segment", "tp", None), P("segment", "tp", None))
    body = shards
    if mesh.shape["tp"] == TP == KV_HEADS and TICKS == 2:
        body = functools.partial(fused, mesh.shape["segment"])
    return jax.shard_map(body, mesh=mesh, in_specs=in_specs, out_specs=out_specs, check_vma=False)
```

```python
import functools
import math

import jax
import jax.numpy as jnp
import numpy as np
from jax import lax
from jax.experimental import pallas as pl
from jax.experimental.pallas import tpu as pltpu
from jax.sharding import PartitionSpec as P

KV_HEADS = 4
HD = 128
SPAN = 128
PREFIX = 1536
TICKS = 2


norm_eps = 1e-05
rope_base = 500000.0


def from_partner(array, axis, stride):
    return lax.ppermute(array, axis, [(i, i ^ 1 << stride) for i in range(lax.axis_size(axis))])


def shifted(block, axis, distance):
    devices = range(lax.axis_size(axis))
    route = [(i - distance, i) for i in devices if i - distance in devices]
    return lax.ppermute(block, axis, route)


def rotate(values, positions):
    half_width = values.shape[-1] // 2
    inverse = rope_base ** (
        -jnp.arange(0, values.shape[-1], 2, dtype=jnp.float32) / values.shape[-1]
    )
    angles = positions.astype(jnp.float32)[:, None] * inverse[None, :]
    cosine_table = jnp.cos(angles)[:, None, :]
    sine_table = jnp.sin(angles)[:, None, :]
    first_half = values[..., :half_width]
    second_half = values[..., half_width:]
    return jnp.concatenate(
        [
            first_half * cosine_table - second_half * sine_table,
            second_half * cosine_table + first_half * sine_table,
        ],
        axis=-1,
    )


def shards(
    residual, pending, span_index, prefix_len, norm_gain, w_query, w_kv, w_out, prefix_cache
):
    group_size = lax.axis_size("tp") // KV_HEADS
    group_bits = group_size.bit_length() - 1
    tp_place = lax.axis_index("tp")
    local_heads = w_query.shape[2] // HD
    weight_query = w_query[0]
    weight_pairs = w_kv[0]
    weight_out = w_out[0]
    query_width = weight_query.shape[1]
    gain_row = norm_gain[0].astype(jnp.float32)
    head_cache = prefix_cache[0]
    for bit_number in range(group_bits):
        partner = from_partner(head_cache, "tp", bit_number)
        lower_half = tp_place // (1 << bit_number) % 2 == 0
        head_cache = jnp.where(
            lower_half,
            jnp.concatenate([head_cache, partner], 0),
            jnp.concatenate([partner, head_cache], 0),
        )
    cache_keys = head_cache[:, :HD]
    cache_values = head_cache[:, HD:]
    slot_index = jnp.arange(PREFIX, dtype=jnp.int32)
    token_index = jnp.arange(SPAN, dtype=jnp.int32)
    causal = token_index[None, :] <= token_index[:, None]
    score_scale = HD ** (-0.5)
    rows_now = residual[0]
    pending_now = pending[0]
    index_now = span_index
    for segment_tick in range(TICKS):
        last_tick = segment_tick + 1 == TICKS
        widths = rows_now.astype(jnp.float32)
        mean_square = jnp.mean(widths * widths, axis=-1, keepdims=True)
        normed = (widths * lax.rsqrt(mean_square + norm_eps) * gain_row).astype(jnp.bfloat16)
        carried = (widths + pending_now.astype(jnp.float32)).astype(jnp.bfloat16)
        block_rows = lax.all_gather(normed, "tp", axis=0, tiled=True)
        projected = jnp.concatenate(
            [
                jnp.dot(block_rows, weight_query, preferred_element_type=jnp.float32),
                jnp.dot(block_rows, weight_pairs, preferred_element_type=jnp.float32),
            ],
            axis=1,
        )
        positions = index_now[0] * SPAN + token_index
        queries = rotate(
            projected[:, :query_width].reshape(SPAN, local_heads, HD), positions
        ).astype(jnp.bfloat16)
        fresh_head = projected[:, query_width:].astype(jnp.bfloat16)
        for bit_number in range(group_bits):
            partner = from_partner(fresh_head, "tp", bit_number)
            lower_half = tp_place // (1 << bit_number) % 2 == 0
            fresh_head = jnp.where(
                lower_half,
                jnp.concatenate([fresh_head, partner], 1),
                jnp.concatenate([partner, fresh_head], 1),
            )
        new_keys = rotate(fresh_head[:, None, :HD].astype(jnp.float32), positions)[:, 0, :].astype(
            jnp.bfloat16
        )
        new_values = fresh_head[:, HD:]
        score_prefix = (
            jnp.einsum("chd,pd->hcp", queries, cache_keys, preferred_element_type=jnp.float32)
            * score_scale
        )
        score_span = (
            jnp.einsum("chd,kd->hck", queries, new_keys, preferred_element_type=jnp.float32)
            * score_scale
        )
        score_prefix = jnp.where(
            (slot_index < prefix_len[0])[None, None, :], score_prefix, -jnp.inf
        )
        score_span = jnp.where(causal[None], score_span, -jnp.inf)
        row_peak = jnp.maximum(
            jnp.max(score_prefix, axis=-1, keepdims=True),
            jnp.max(score_span, axis=-1, keepdims=True),
        )
        exp_prefix = jnp.exp(score_prefix - row_peak)
        exp_span = jnp.exp(score_span - row_peak)
        denominator = jnp.sum(exp_prefix, axis=-1, keepdims=True) + jnp.sum(
            exp_span, axis=-1, keepdims=True
        )
        weight_prefix = (exp_prefix / denominator).astype(jnp.bfloat16)
        weight_span = (exp_span / denominator).astype(jnp.bfloat16)
        attended = jnp.einsum(
            "hcp,pd->chd", weight_prefix, cache_values, preferred_element_type=jnp.float32
        )
        attended = attended + jnp.einsum(
            "hck,kd->chd", weight_span, new_values, preferred_element_type=jnp.float32
        )
        attended = attended.astype(jnp.bfloat16).reshape(SPAN, local_heads * HD)
        summed = lax.psum_scatter(
            jnp.dot(attended, weight_out, preferred_element_type=jnp.float32),
            "tp",
            scatter_dimension=0,
            tiled=True,
        )
        output = summed.astype(jnp.bfloat16)
        if not last_tick:
            rows_now, pending_now, index_now = shifted((carried, output, index_now), "segment", 1)
    return (carried[None], output[None])


TP = 4
ROWS = SPAN // TP
HALF = 2 * ROWS
PIECE = ROWS // 2
OUT_CHUNKS = 4
TILE = 256
WIDE = 512
MASKED = -1e30


def fused_kernel(
    sections,
    span_ref,
    len_ref,
    residual_hbm,
    pending_hbm,
    gain_hbm,
    w_query_hbm,
    w_kv_hbm,
    w_out_hbm,
    cache_hbm,
    carried_ref,
    output_ref,
    residual,
    pending,
    gain_ref,
    w_query,
    w_kv,
    w_out,
    keys,
    values,
    span_keys,
    span_values,
    tokens,
    carried_own,
    carried_in,
    index_own,
    index_in,
    cosines,
    sines,
    projected,
    queries,
    peaks,
    totals,
    mixes,
    attended,
    partial,
    pair_send,
    pair_recv,
    far_send,
    far_recv,
    first_out,
    out_in,
    row_sem,
    load_sem,
    gather_send,
    gather_recv,
    shift_send,
    shift_recv,
    pair_send_sem,
    pair_recv_sem,
    far_send_sem,
    far_recv_sem,
    out_send_sem,
    out_recv_sem,
):
    features = w_query.shape[0]
    query_width = w_query.shape[1]
    heads = query_width // HD
    chunk = features // OUT_CHUNKS
    seg = lax.axis_index("segment")
    me = lax.axis_index("tp")
    core = lax.rem(me, 2)
    side = me // 2
    pair = me + 1 - 2 * core
    far = lax.rem(me + 2, TP)
    has_prev = seg > 0
    has_next = seg < sections - 1

    barrier = pltpu.get_barrier_semaphore()
    for partner in (pair, far):
        pl.semaphore_signal(barrier, inc=1, device_id={"tp": partner})

    @pl.when(has_prev)
    def _():
        pl.semaphore_signal(barrier, inc=1, device_id={"segment": seg - 1})

    @pl.when(has_next)
    def _():
        pl.semaphore_signal(barrier, inc=1, device_id={"segment": seg + 1})

    row_loads = [
        pltpu.make_async_copy(residual_hbm.at[0], residual, row_sem.at[0]),
        pltpu.make_async_copy(gain_hbm, gain_ref, row_sem.at[2]),
        pltpu.make_async_copy(pending_hbm.at[0], pending, row_sem.at[1]),
    ]
    loads = []
    quarter = features // 4
    for part in range(4):
        span = pl.ds(part * quarter, quarter)
        loads.append((w_query_hbm.at[0, span], w_query.at[span]))
    loads.append((w_kv_hbm.at[0], w_kv))
    loads.append((cache_hbm.at[0, :, pl.ds(0, HD)], keys))
    loads.append((cache_hbm.at[0, :, pl.ds(HD, HD)], values))
    quarter_out = query_width // 4
    for part in range(4):
        span = pl.ds(part * quarter_out, quarter_out)
        loads.append((w_out_hbm.at[0, span], w_out.at[span]))
    loads = [
        pltpu.make_async_copy(source, target, load_sem.at[number])
        for number, (source, target) in enumerate(loads)
    ]
    for load in row_loads:
        load.start()

    def rows_of(slot, which, part=None):
        if part is None:
            return pl.ds(pl.multiple_of(slot * HALF + which * ROWS, ROWS), ROWS)
        return pl.ds(pl.multiple_of(slot * HALF + which * ROWS + part * PIECE, PIECE), PIECE)

    def normed(rows):
        widths = rows.astype(jnp.float32)
        gain = gain_ref[...].astype(jnp.float32)
        mean_square = jnp.mean(widths * widths, axis=-1, keepdims=True)
        return (widths * lax.rsqrt(mean_square + norm_eps) * gain).astype(jnp.bfloat16)

    def gather_copy(tick, leg, part):
        here, there = ((0, 1), (0, 0), (1, 1))[leg]
        return pltpu.make_async_remote_copy(
            src_ref=tokens.at[rows_of(2 * tick + here, core, part)],
            dst_ref=tokens.at[rows_of(2 * tick + there, core, part)],
            send_sem=gather_send.at[tick, leg, part],
            recv_sem=gather_recv.at[tick, leg, part],
            device_id={"tp": far if leg == 0 else pair},
        )

    def shift_copy(part):
        rows = pl.ds(part * PIECE, PIECE)
        return pltpu.make_async_remote_copy(
            src_ref=carried_own.at[rows],
            dst_ref=carried_in.at[rows],
            send_sem=shift_send.at[part],
            recv_sem=shift_recv.at[part],
            device_id={"segment": seg + 1},
        )

    def index_copy():
        return pltpu.make_async_remote_copy(
            src_ref=index_own,
            dst_ref=index_in,
            send_sem=shift_send.at[2],
            recv_sem=shift_recv.at[2],
            device_id={"segment": seg + 1},
        )

    def pair_copy(tick, number, kind):
        return pltpu.make_async_remote_copy(
            src_ref=pair_send.at[tick, number, kind],
            dst_ref=pair_recv.at[tick, number, kind],
            send_sem=pair_send_sem.at[tick, number, kind],
            recv_sem=pair_recv_sem.at[tick, number, kind],
            device_id={"tp": pair},
        )

    def far_copy(tick, number):
        return pltpu.make_async_remote_copy(
            src_ref=far_send.at[tick, number],
            dst_ref=far_recv.at[tick, number],
            send_sem=far_send_sem.at[tick, number],
            recv_sem=far_recv_sem.at[tick, number],
            device_id={"tp": far},
        )

    def out_copy(number):
        return pltpu.make_async_remote_copy(
            src_ref=first_out.at[number],
            dst_ref=out_in.at[number],
            send_sem=out_send_sem.at[number],
            recv_sem=out_recv_sem.at[number],
            device_id={"segment": seg + 1},
        )

    row_loads[0].wait()
    row_loads[1].wait()
    for load in loads[:5]:
        load.start()
    for part in range(2):
        tokens[rows_of(0, core, part)] = normed(residual[part * PIECE : (part + 1) * PIECE])
        if part == 0:
            pl.semaphore_wait(barrier, 2 + has_prev.astype(jnp.int32) + has_next.astype(jnp.int32))
        gather_copy(0, 0, part).start()
    row_loads[2].wait()
    carried_own[...] = (
        residual[...].astype(jnp.float32) + pending[...].astype(jnp.float32)
    ).astype(jnp.bfloat16)
    index_own[...] = jnp.full(index_own.shape, span_ref[0], jnp.int32)

    @pl.when(has_next)
    def _():
        for part in range(2):
            shift_copy(part).start()
        index_copy().start()

    for part in range(2):
        gather_copy(0, 1, part).start()
    for load in loads[5:]:
        load.start()

    @pl.when(jnp.logical_not(has_prev))
    def _():
        carried_in[...] = jnp.zeros_like(carried_in)
        index_in[...] = jnp.zeros_like(index_in)
        out_in[...] = jnp.zeros_like(out_in)

    lane = lax.broadcasted_iota(jnp.int32, (SPAN, HD), 1)
    token = (lax.broadcasted_iota(jnp.int32, (SPAN, HD), 0) + side * HALF) & (SPAN - 1)
    inverse = jnp.zeros((1, HD), jnp.float32)
    frequencies = (rope_base ** (-np.arange(0, HD, 2, dtype=np.float64) / HD)).astype(np.float32)
    for place, frequency in enumerate(frequencies):
        inverse = jnp.where(lane[0:1] % (HD // 2) == place, float(frequency), inverse)
    key_token = (lane + side * HALF) & (SPAN - 1)

    def tables(tick, index_tile):
        positions = (index_tile[0:1, :] * SPAN + token).astype(jnp.float32)
        angles = positions * inverse
        sine = jnp.sin(angles)
        cosines[tick] = jnp.cos(angles)
        sines[tick] = jnp.where(lane < HD // 2, -sine, sine)

    def rotated(block, slot):
        tick, half = slot // 2, slot % 2
        rows = slice(half * HALF, (half + 1) * HALF)
        turned = pltpu.roll(block, HD // 2, 1)
        return (block * cosines[tick, rows] + turned * sines[tick, rows]).astype(jnp.bfloat16)

    causal_bias = jnp.where(key_token <= token, 0.0, MASKED).astype(jnp.float32)
    group = TILE // HALF
    slot_index = lax.broadcasted_iota(jnp.int32, (1, PREFIX), 1)
    slot_bias = jnp.where(slot_index < len_ref[0], 0.0, MASKED).astype(jnp.float32)
    score_scale = HD ** (-0.5) * math.log2(math.e)
    transposed = (((1,), (1,)), ((), ()))

    def relay(tick, part):
        gather_copy(tick, 0, part).wait_recv()
        gather_copy(tick, 2, part).start()

    def take_shifted(part):
        @pl.when(has_prev)
        def _():
            shift_copy(part).wait_recv()

        rows = carried_in[part * PIECE : (part + 1) * PIECE]
        tokens[rows_of(2, core, part)] = normed(rows)
        gather_copy(1, 0, part).start()
        gather_copy(1, 1, part).start()

    def project(slots):
        first, count = slots[0] * HALF, len(slots) * HALF

        def tile(number, carry):
            columns = pl.ds(pl.multiple_of(number * WIDE, WIDE), WIDE)
            projected[:count, columns] = jnp.dot(
                tokens[first : first + count], w_query[:, columns], preferred_element_type=jnp.float32
            )
            return carry

        lax.fori_loop(0, query_width // WIDE, tile, 0)
        projected[:count, query_width:] = jnp.dot(
            tokens[first : first + count], w_kv[...], preferred_element_type=jnp.float32
        )

    def spread(slots):
        for place, slot in enumerate(slots):
            rows = slice(place * HALF, (place + 1) * HALF)
            for head in range(heads):
                block = projected[rows, head * HD : (head + 1) * HD]
                queries[slot, head * HALF : (head + 1) * HALF] = rotated(block, slot)
            tick, half = slot // 2, slot % 2
            span = slice(half * HALF, (half + 1) * HALF)
            fresh = projected[rows, query_width : query_width + HD].astype(jnp.bfloat16)
            span_keys[tick, span] = rotated(fresh.astype(jnp.float32), slot)
            span_values[tick, span] = projected[rows, query_width + HD :].astype(jnp.bfloat16)

    def attend_prefix(slot):
        half = slot % 2
        for block in range(heads // group):
            rows = slice(block * TILE, (block + 1) * TILE)
            scores = lax.dot_general(
                queries[slot, rows], keys[...], transposed, preferred_element_type=jnp.float32
            )
            scores = scores * score_scale + slot_bias
            peak = jnp.max(scores, axis=-1, keepdims=True)
            weights = jnp.exp2(scores - peak)
            total = jnp.sum(weights, axis=-1, keepdims=True)
            mixes[half, rows] = jnp.dot(
                weights.astype(jnp.bfloat16), values[...], preferred_element_type=jnp.float32
            )
            peaks[half, rows] = jnp.broadcast_to(peak, (TILE, HD))
            totals[half, rows] = jnp.broadcast_to(total, (TILE, HD))

    def attend_span(slot):
        tick, half = slot // 2, slot % 2
        bias = causal_bias[half * HALF : (half + 1) * HALF]
        bias = jnp.concatenate([bias] * group, 0)
        for block in range(heads // group):
            rows = slice(block * TILE, (block + 1) * TILE)
            scores = lax.dot_general(
                queries[slot, rows], span_keys[tick], transposed, preferred_element_type=jnp.float32
            )
            scores = scores * score_scale + bias
            before = peaks[half, rows]
            peak = jnp.maximum(before, jnp.max(scores, axis=-1, keepdims=True))
            weights = jnp.exp2(scores - peak)
            shrink = jnp.exp2(before - peak)
            fresh = jnp.dot(
                weights.astype(jnp.bfloat16), span_values[tick], preferred_element_type=jnp.float32
            )
            total = totals[half, rows] * shrink + jnp.sum(weights, axis=-1, keepdims=True)
            mixed = mixes[half, rows] * shrink + fresh
            mixed = (mixed / total).astype(jnp.bfloat16)
            for place in range(group):
                head = block * group + place
                attended[half * HALF : (half + 1) * HALF, head * HD : (head + 1) * HD] = mixed[
                    place * HALF : (place + 1) * HALF
                ]

    def pass_on(tick, number):
        columns = slice(number * chunk, (number + 1) * chunk)
        pair_copy(tick, number, 1).wait_recv()
        far_send[tick, number] = (
            partial[rows_of(1, core), columns] + pair_recv[tick, number, 1].astype(jnp.float32)
        ).astype(jnp.bfloat16)
        far_copy(tick, number).start()

    def emit(tick, halves):
        first, last = halves[0] * HALF, (halves[-1] + 1) * HALF
        for number in range(OUT_CHUNKS):
            columns = slice(number * chunk, (number + 1) * chunk)
            partial[first:last, columns] = jnp.dot(
                attended[first:last], w_out[:, columns], preferred_element_type=jnp.float32
            )
            for kind in reversed(halves):
                pair_send[tick, number, kind] = partial[rows_of(kind, 1 - core), columns].astype(
                    jnp.bfloat16
                )
                pair_copy(tick, number, kind).start()
            if 1 in halves and number > 1:
                pass_on(tick, number - 2)
        if 1 in halves:
            for number in range(OUT_CHUNKS - 2, OUT_CHUNKS):
                pass_on(tick, number)

    def summed(tick, number):
        columns = slice(number * chunk, (number + 1) * chunk)
        pair_copy(tick, number, 0).wait_recv()
        beside = partial[rows_of(0, core), columns] + pair_recv[tick, number, 0].astype(jnp.float32)
        far_copy(tick, number).wait_recv()
        return (beside + far_recv[tick, number].astype(jnp.float32)).astype(jnp.bfloat16)

    def finish_first(number):
        first_out[number] = summed(0, number)

        @pl.when(has_next)
        def _():
            out_copy(number).start()

    tables(0, index_own[...])
    for part in range(2):
        gather_copy(0, 1, part).wait_recv()
    for load in loads[:5]:
        load.wait()
    project((0,))
    relay(0, 0)
    spread((0,))
    for load in loads[5:7]:
        load.wait()
    attend_prefix(0)
    relay(0, 1)
    take_shifted(0)
    for part in range(2):
        gather_copy(0, 2, part).wait_recv()
    project((1,))
    take_shifted(1)
    spread((1,))
    attend_prefix(1)
    attend_span(1)
    attend_span(0)
    for load in loads[7:]:
        load.wait()
    for part in range(2):
        relay(1, part)
    emit(0, (0, 1))

    @pl.when(has_prev)
    def _():
        index_copy().wait_recv()

    tables(1, index_in[...])
    for part in range(2):
        gather_copy(1, 1, part).wait_recv()
        gather_copy(1, 2, part).wait_recv()
    project((2, 3))
    spread((2, 3))
    attend_prefix(3)
    attend_span(3)
    for number in range(OUT_CHUNKS // 2):
        finish_first(number)
    emit(1, (1,))
    for number in range(OUT_CHUNKS // 2, OUT_CHUNKS):
        finish_first(number)
    attend_prefix(2)
    attend_span(2)
    emit(1, (0,))
    for number in range(OUT_CHUNKS):
        columns = slice(number * chunk, (number + 1) * chunk)
        output_ref[0, :, columns] = summed(1, number)
    for number in range(OUT_CHUNKS):
        columns = slice(number * chunk, (number + 1) * chunk)

        @pl.when(has_prev)
        def _():
            out_copy(number).wait_recv()

        carried_ref[0, :, columns] = (
            carried_in[:, columns].astype(jnp.float32) + out_in[number].astype(jnp.float32)
        ).astype(jnp.bfloat16)

    for tick in range(2):
        for part in range(2):
            for leg in range(3):
                gather_copy(tick, leg, part).wait_send()
        for number in range(OUT_CHUNKS):
            for kind in range(2):
                pair_copy(tick, number, kind).wait_send()
            far_copy(tick, number).wait_send()

    @pl.when(has_next)
    def _():
        for part in range(2):
            shift_copy(part).wait_send()
        index_copy().wait_send()
        for number in range(OUT_CHUNKS):
            out_copy(number).wait_send()


def hand_out_kernel(carried_from, output_from, carried_to, output_to, sem):
    rows = carried_from.shape[1] // 2
    copies = [
        pltpu.make_async_copy(
            source.at[0, pl.ds(part * rows, rows)],
            target.at[0, pl.ds(part * rows, rows)],
            sem.at[place, part],
        )
        for place, (source, target) in enumerate(
            ((carried_from, carried_to), (output_from, output_to))
        )
        for part in range(2)
    ]
    for copy in copies:
        copy.start()
    for copy in copies:
        copy.wait()


def hand_out(carried, output):
    near = pl.BlockSpec(memory_space=pltpu.VMEM)
    whole = pl.BlockSpec(memory_space=pl.ANY)
    shape = jax.ShapeDtypeStruct(carried.shape, carried.dtype)
    return pl.pallas_call(
        hand_out_kernel,
        out_shape=(shape, shape),
        in_specs=[near, near],
        out_specs=(whole, whole),
        scratch_shapes=[pltpu.SemaphoreType.DMA((2, 2))],
        compiler_params=pltpu.CompilerParams(vmem_limit_bytes=4 * 1024 * 1024),
        name="hand_out",
    )(carried, output)


def fused(
    sections,
    residual,
    pending,
    span_index,
    prefix_len,
    norm_gain,
    w_query,
    w_kv,
    w_out,
    prefix_cache,
):
    features, query_width = w_query.shape[1:]
    pair_width = w_kv.shape[2]
    chunk = features // OUT_CHUNKS
    smem = pl.BlockSpec(memory_space=pltpu.SMEM)
    vmem = pl.BlockSpec(memory_space=pltpu.VMEM)
    whole = pl.BlockSpec(memory_space=pl.ANY)
    half = jnp.bfloat16
    dma = pltpu.SemaphoreType.DMA
    carried, output = pl.pallas_call(
        functools.partial(fused_kernel, sections),
        out_shape=(
            jax.ShapeDtypeStruct(residual.shape, half),
            jax.ShapeDtypeStruct(residual.shape, half),
        ),
        in_specs=[smem, smem] + [whole] * 7,
        out_specs=(vmem, vmem),
        scratch_shapes=[
            pltpu.VMEM((ROWS, features), half),
            pltpu.VMEM((ROWS, features), half),
            pltpu.VMEM((1, features), half),
            pltpu.VMEM((features, query_width), half),
            pltpu.VMEM((features, pair_width), half),
            pltpu.VMEM((query_width, features), half),
            pltpu.VMEM((PREFIX, HD), half),
            pltpu.VMEM((PREFIX, HD), half),
            pltpu.VMEM((2, SPAN, HD), half),
            pltpu.VMEM((2, SPAN, HD), half),
            pltpu.VMEM((2 * SPAN, features), half),
            pltpu.VMEM((ROWS, features), half),
            pltpu.VMEM((ROWS, features), half),
            pltpu.VMEM((8, HD), jnp.int32),
            pltpu.VMEM((8, HD), jnp.int32),
            pltpu.VMEM((2, SPAN, HD), jnp.float32),
            pltpu.VMEM((2, SPAN, HD), jnp.float32),
            pltpu.VMEM((SPAN, query_width + pair_width), jnp.float32),
            pltpu.VMEM((4, query_width // HD * HALF, HD), half),
            pltpu.VMEM((2, query_width // HD * HALF, HD), jnp.float32),
            pltpu.VMEM((2, query_width // HD * HALF, HD), jnp.float32),
            pltpu.VMEM((2, query_width // HD * HALF, HD), jnp.float32),
            pltpu.VMEM((SPAN, query_width), half),
            pltpu.VMEM((SPAN, features), jnp.float32),
            pltpu.VMEM((2, OUT_CHUNKS, 2, ROWS, chunk), half),
            pltpu.VMEM((2, OUT_CHUNKS, 2, ROWS, chunk), half),
            pltpu.VMEM((2, OUT_CHUNKS, ROWS, chunk), half),
            pltpu.VMEM((2, OUT_CHUNKS, ROWS, chunk), half),
            pltpu.VMEM((OUT_CHUNKS, ROWS, chunk), half),
            pltpu.VMEM((OUT_CHUNKS, ROWS, chunk), half),
            dma((3,)),
            dma((11,)),
            dma((2, 3, 2)),
            dma((2, 3, 2)),
            dma((3,)),
            dma((3,)),
            dma((2, OUT_CHUNKS, 2)),
            dma((2, OUT_CHUNKS, 2)),
            dma((2, OUT_CHUNKS)),
            dma((2, OUT_CHUNKS)),
            dma((OUT_CHUNKS,)),
            dma((OUT_CHUNKS,)),
        ],
        compiler_params=pltpu.CompilerParams(
            collective_id=0, has_side_effects=True, vmem_limit_bytes=54528 * 1024
        ),
        name="fused_relay",
    )(
        span_index,
        prefix_len,
        residual,
        pending,
        norm_gain,
        w_query,
        w_kv,
        w_out,
        prefix_cache,
    )
    return hand_out(carried, output)


def solution(mesh):
    in_specs = (
        P("segment", "tp", None),
        P("segment", "tp", None),
        P("segment"),
        P("segment"),
        P("segment", None),
        P("segment", None, "tp"),
        P("segment", None, "tp"),
        P("segment", "tp", None),
        P("segment", "tp", None),
    )
    out_specs = (P("segment", "tp", None), P("segment", "tp", None))
    body = shards
    if mesh.shape["tp"] == TP == KV_HEADS and TICKS == 2:
        body = functools.partial(fused, mesh.shape["segment"])
    return jax.shard_map(body, mesh=mesh, in_specs=in_specs, out_specs=out_specs, check_vma=False)
```

```python
import functools
import math

import jax
import jax.numpy as jnp
import numpy as np
from jax import lax
from jax.experimental import pallas as pl
from jax.experimental.pallas import tpu as pltpu
from jax.sharding import PartitionSpec as P

KV_HEADS = 4
HD = 128
SPAN = 128
PREFIX = 1536
TICKS = 2


norm_eps = 1e-05
rope_base = 500000.0


def from_partner(array, axis, stride):
    return lax.ppermute(array, axis, [(i, i ^ 1 << stride) for i in range(lax.axis_size(axis))])


def shifted(block, axis, distance):
    devices = range(lax.axis_size(axis))
    route = [(i - distance, i) for i in devices if i - distance in devices]
    return lax.ppermute(block, axis, route)


def rotate(values, positions):
    half_width = values.shape[-1] // 2
    inverse = rope_base ** (
        -jnp.arange(0, values.shape[-1], 2, dtype=jnp.float32) / values.shape[-1]
    )
    angles = positions.astype(jnp.float32)[:, None] * inverse[None, :]
    cosine_table = jnp.cos(angles)[:, None, :]
    sine_table = jnp.sin(angles)[:, None, :]
    first_half = values[..., :half_width]
    second_half = values[..., half_width:]
    return jnp.concatenate(
        [
            first_half * cosine_table - second_half * sine_table,
            second_half * cosine_table + first_half * sine_table,
        ],
        axis=-1,
    )


def shards(
    residual, pending, span_index, prefix_len, norm_gain, w_query, w_kv, w_out, prefix_cache
):
    group_size = lax.axis_size("tp") // KV_HEADS
    group_bits = group_size.bit_length() - 1
    tp_place = lax.axis_index("tp")
    local_heads = w_query.shape[2] // HD
    weight_query = w_query[0]
    weight_pairs = w_kv[0]
    weight_out = w_out[0]
    query_width = weight_query.shape[1]
    gain_row = norm_gain[0].astype(jnp.float32)
    head_cache = prefix_cache[0]
    for bit_number in range(group_bits):
        partner = from_partner(head_cache, "tp", bit_number)
        lower_half = tp_place // (1 << bit_number) % 2 == 0
        head_cache = jnp.where(
            lower_half,
            jnp.concatenate([head_cache, partner], 0),
            jnp.concatenate([partner, head_cache], 0),
        )
    cache_keys = head_cache[:, :HD]
    cache_values = head_cache[:, HD:]
    slot_index = jnp.arange(PREFIX, dtype=jnp.int32)
    token_index = jnp.arange(SPAN, dtype=jnp.int32)
    causal = token_index[None, :] <= token_index[:, None]
    score_scale = HD ** (-0.5)
    rows_now = residual[0]
    pending_now = pending[0]
    index_now = span_index
    for segment_tick in range(TICKS):
        last_tick = segment_tick + 1 == TICKS
        widths = rows_now.astype(jnp.float32)
        mean_square = jnp.mean(widths * widths, axis=-1, keepdims=True)
        normed = (widths * lax.rsqrt(mean_square + norm_eps) * gain_row).astype(jnp.bfloat16)
        carried = (widths + pending_now.astype(jnp.float32)).astype(jnp.bfloat16)
        block_rows = lax.all_gather(normed, "tp", axis=0, tiled=True)
        projected = jnp.concatenate(
            [
                jnp.dot(block_rows, weight_query, preferred_element_type=jnp.float32),
                jnp.dot(block_rows, weight_pairs, preferred_element_type=jnp.float32),
            ],
            axis=1,
        )
        positions = index_now[0] * SPAN + token_index
        queries = rotate(
            projected[:, :query_width].reshape(SPAN, local_heads, HD), positions
        ).astype(jnp.bfloat16)
        fresh_head = projected[:, query_width:].astype(jnp.bfloat16)
        for bit_number in range(group_bits):
            partner = from_partner(fresh_head, "tp", bit_number)
            lower_half = tp_place // (1 << bit_number) % 2 == 0
            fresh_head = jnp.where(
                lower_half,
                jnp.concatenate([fresh_head, partner], 1),
                jnp.concatenate([partner, fresh_head], 1),
            )
        new_keys = rotate(fresh_head[:, None, :HD].astype(jnp.float32), positions)[:, 0, :].astype(
            jnp.bfloat16
        )
        new_values = fresh_head[:, HD:]
        score_prefix = (
            jnp.einsum("chd,pd->hcp", queries, cache_keys, preferred_element_type=jnp.float32)
            * score_scale
        )
        score_span = (
            jnp.einsum("chd,kd->hck", queries, new_keys, preferred_element_type=jnp.float32)
            * score_scale
        )
        score_prefix = jnp.where(
            (slot_index < prefix_len[0])[None, None, :], score_prefix, -jnp.inf
        )
        score_span = jnp.where(causal[None], score_span, -jnp.inf)
        row_peak = jnp.maximum(
            jnp.max(score_prefix, axis=-1, keepdims=True),
            jnp.max(score_span, axis=-1, keepdims=True),
        )
        exp_prefix = jnp.exp(score_prefix - row_peak)
        exp_span = jnp.exp(score_span - row_peak)
        denominator = jnp.sum(exp_prefix, axis=-1, keepdims=True) + jnp.sum(
            exp_span, axis=-1, keepdims=True
        )
        weight_prefix = (exp_prefix / denominator).astype(jnp.bfloat16)
        weight_span = (exp_span / denominator).astype(jnp.bfloat16)
        attended = jnp.einsum(
            "hcp,pd->chd", weight_prefix, cache_values, preferred_element_type=jnp.float32
        )
        attended = attended + jnp.einsum(
            "hck,kd->chd", weight_span, new_values, preferred_element_type=jnp.float32
        )
        attended = attended.astype(jnp.bfloat16).reshape(SPAN, local_heads * HD)
        summed = lax.psum_scatter(
            jnp.dot(attended, weight_out, preferred_element_type=jnp.float32),
            "tp",
            scatter_dimension=0,
            tiled=True,
        )
        output = summed.astype(jnp.bfloat16)
        if not last_tick:
            rows_now, pending_now, index_now = shifted((carried, output, index_now), "segment", 1)
    return (carried[None], output[None])


TP = 4
ROWS = SPAN // TP
HALF = 2 * ROWS
PIECE = ROWS // 2
OUT_CHUNKS = 4
TILE = 256
WIDE = 512
MASKED = -1e30


def fused_kernel(
    sections,
    span_ref,
    len_ref,
    residual_hbm,
    pending_hbm,
    gain_hbm,
    w_query_hbm,
    w_kv_hbm,
    w_out_hbm,
    cache_hbm,
    carried_ref,
    output_ref,
    residual,
    pending,
    gain_ref,
    w_query,
    w_kv,
    w_out,
    keys,
    values,
    span_keys,
    span_values,
    tokens,
    carried_own,
    carried_in,
    index_own,
    index_in,
    cosines,
    sines,
    projected,
    queries,
    peaks,
    totals,
    mixes,
    attended,
    partial,
    pair_send,
    pair_recv,
    far_send,
    far_recv,
    first_out,
    out_in,
    row_sem,
    load_sem,
    gather_send,
    gather_recv,
    shift_send,
    shift_recv,
    pair_send_sem,
    pair_recv_sem,
    far_send_sem,
    far_recv_sem,
    out_send_sem,
    out_recv_sem,
):
    features = w_query.shape[0]
    query_width = w_query.shape[1]
    heads = query_width // HD
    chunk = features // OUT_CHUNKS
    seg = lax.axis_index("segment")
    me = lax.axis_index("tp")
    core = lax.rem(me, 2)
    side = me // 2
    pair = me + 1 - 2 * core
    far = lax.rem(me + 2, TP)
    has_prev = seg > 0
    has_next = seg < sections - 1

    barrier = pltpu.get_barrier_semaphore()
    for partner in (pair, far):
        pl.semaphore_signal(barrier, inc=1, device_id={"tp": partner})

    @pl.when(has_prev)
    def _():
        pl.semaphore_signal(barrier, inc=1, device_id={"segment": seg - 1})

    @pl.when(has_next)
    def _():
        pl.semaphore_signal(barrier, inc=1, device_id={"segment": seg + 1})

    row_loads = [
        pltpu.make_async_copy(residual_hbm.at[0], residual, row_sem.at[0]),
        pltpu.make_async_copy(gain_hbm, gain_ref, row_sem.at[2]),
        pltpu.make_async_copy(pending_hbm.at[0], pending, row_sem.at[1]),
    ]
    loads = []
    quarter = features // 4
    for part in range(4):
        span = pl.ds(part * quarter, quarter)
        loads.append((w_query_hbm.at[0, span], w_query.at[span]))
    loads.append((w_kv_hbm.at[0], w_kv))
    loads.append((cache_hbm.at[0, :, pl.ds(0, HD)], keys))
    loads.append((cache_hbm.at[0, :, pl.ds(HD, HD)], values))
    quarter_out = query_width // 4
    for part in range(4):
        span = pl.ds(part * quarter_out, quarter_out)
        loads.append((w_out_hbm.at[0, span], w_out.at[span]))
    loads = [
        pltpu.make_async_copy(source, target, load_sem.at[number])
        for number, (source, target) in enumerate(loads)
    ]
    for load in row_loads:
        load.start()

    def rows_of(slot, which, part=None):
        if part is None:
            return pl.ds(pl.multiple_of(slot * HALF + which * ROWS, ROWS), ROWS)
        return pl.ds(pl.multiple_of(slot * HALF + which * ROWS + part * PIECE, PIECE), PIECE)

    def normed(rows):
        widths = rows.astype(jnp.float32)
        gain = gain_ref[...].astype(jnp.float32)
        mean_square = jnp.mean(widths * widths, axis=-1, keepdims=True)
        return (widths * lax.rsqrt(mean_square + norm_eps) * gain).astype(jnp.bfloat16)

    def gather_copy(tick, leg, part):
        here, there = ((0, 1), (0, 0), (1, 1))[leg]
        return pltpu.make_async_remote_copy(
            src_ref=tokens.at[rows_of(2 * tick + here, core, part)],
            dst_ref=tokens.at[rows_of(2 * tick + there, core, part)],
            send_sem=gather_send.at[tick, leg, part],
            recv_sem=gather_recv.at[tick, leg, part],
            device_id={"tp": far if leg == 0 else pair},
        )

    def shift_copy(part):
        rows = pl.ds(part * PIECE, PIECE)
        return pltpu.make_async_remote_copy(
            src_ref=carried_own.at[rows],
            dst_ref=carried_in.at[rows],
            send_sem=shift_send.at[part],
            recv_sem=shift_recv.at[part],
            device_id={"segment": seg + 1},
        )

    def index_copy():
        return pltpu.make_async_remote_copy(
            src_ref=index_own,
            dst_ref=index_in,
            send_sem=shift_send.at[2],
            recv_sem=shift_recv.at[2],
            device_id={"segment": seg + 1},
        )

    def pair_copy(tick, number, kind):
        return pltpu.make_async_remote_copy(
            src_ref=pair_send.at[tick, number, kind],
            dst_ref=pair_recv.at[tick, number, kind],
            send_sem=pair_send_sem.at[tick, number, kind],
            recv_sem=pair_recv_sem.at[tick, number, kind],
            device_id={"tp": pair},
        )

    def far_copy(tick, number):
        return pltpu.make_async_remote_copy(
            src_ref=far_send.at[tick, number],
            dst_ref=far_recv.at[tick, number],
            send_sem=far_send_sem.at[tick, number],
            recv_sem=far_recv_sem.at[tick, number],
            device_id={"tp": far},
        )

    def out_copy(number):
        return pltpu.make_async_remote_copy(
            src_ref=first_out.at[number],
            dst_ref=out_in.at[number],
            send_sem=out_send_sem.at[number],
            recv_sem=out_recv_sem.at[number],
            device_id={"segment": seg + 1},
        )

    row_loads[0].wait()
    row_loads[1].wait()
    for load in loads:
        load.start()
    for part in range(2):
        tokens[rows_of(0, core, part)] = normed(residual[part * PIECE : (part + 1) * PIECE])
        if part == 0:
            pl.semaphore_wait(barrier, 2 + has_prev.astype(jnp.int32) + has_next.astype(jnp.int32))
        gather_copy(0, 0, part).start()
    row_loads[2].wait()
    carried_own[...] = (
        residual[...].astype(jnp.float32) + pending[...].astype(jnp.float32)
    ).astype(jnp.bfloat16)
    index_own[...] = jnp.full(index_own.shape, span_ref[0], jnp.int32)

    @pl.when(has_next)
    def _():
        for part in range(2):
            shift_copy(part).start()
        index_copy().start()

    for part in range(2):
        gather_copy(0, 1, part).start()

    @pl.when(jnp.logical_not(has_prev))
    def _():
        carried_in[...] = jnp.zeros_like(carried_in)
        index_in[...] = jnp.zeros_like(index_in)
        out_in[...] = jnp.zeros_like(out_in)

    lane = lax.broadcasted_iota(jnp.int32, (SPAN, HD), 1)
    token = (lax.broadcasted_iota(jnp.int32, (SPAN, HD), 0) + side * HALF) & (SPAN - 1)
    inverse = jnp.zeros((1, HD), jnp.float32)
    frequencies = (rope_base ** (-np.arange(0, HD, 2, dtype=np.float64) / HD)).astype(np.float32)
    for place, frequency in enumerate(frequencies):
        inverse = jnp.where(lane[0:1] % (HD // 2) == place, float(frequency), inverse)
    key_token = (lane + side * HALF) & (SPAN - 1)

    def tables(tick, index_tile):
        positions = (index_tile[0:1, :] * SPAN + token).astype(jnp.float32)
        angles = positions * inverse
        sine = jnp.sin(angles)
        cosines[tick] = jnp.cos(angles)
        sines[tick] = jnp.where(lane < HD // 2, -sine, sine)

    def rotated(block, slot):
        tick, half = slot // 2, slot % 2
        rows = slice(half * HALF, (half + 1) * HALF)
        turned = pltpu.roll(block, HD // 2, 1)
        return (block * cosines[tick, rows] + turned * sines[tick, rows]).astype(jnp.bfloat16)

    causal_bias = jnp.where(key_token <= token, 0.0, MASKED).astype(jnp.float32)
    group = TILE // HALF
    slot_index = lax.broadcasted_iota(jnp.int32, (1, PREFIX), 1)
    slot_bias = jnp.where(slot_index < len_ref[0], 0.0, MASKED).astype(jnp.float32)
    score_scale = HD ** (-0.5) * math.log2(math.e)
    transposed = (((1,), (1,)), ((), ()))

    def relay_and_shift(part):
        gather_copy(0, 0, part).wait_recv()
        gather_copy(0, 2, part).start()

        @pl.when(has_prev)
        def _():
            shift_copy(part).wait_recv()

        rows = carried_in[part * PIECE : (part + 1) * PIECE]
        tokens[rows_of(2, core, part)] = normed(rows)
        gather_copy(1, 0, part).start()
        gather_copy(1, 1, part).start()

    def project(slots):
        first, count = slots[0] * HALF, len(slots) * HALF

        def tile(number, carry):
            columns = pl.ds(pl.multiple_of(number * WIDE, WIDE), WIDE)
            projected[:count, columns] = jnp.dot(
                tokens[first : first + count], w_query[:, columns], preferred_element_type=jnp.float32
            )
            return carry

        lax.fori_loop(0, query_width // WIDE, tile, 0)
        projected[:count, query_width:] = jnp.dot(
            tokens[first : first + count], w_kv[...], preferred_element_type=jnp.float32
        )

    def spread(slots):
        for place, slot in enumerate(slots):
            rows = slice(place * HALF, (place + 1) * HALF)
            for head in range(heads):
                block = projected[rows, head * HD : (head + 1) * HD]
                queries[slot, head * HALF : (head + 1) * HALF] = rotated(block, slot)
            tick, half = slot // 2, slot % 2
            span = slice(half * HALF, (half + 1) * HALF)
            fresh = projected[rows, query_width : query_width + HD].astype(jnp.bfloat16)
            span_keys[tick, span] = rotated(fresh.astype(jnp.float32), slot)
            span_values[tick, span] = projected[rows, query_width + HD :].astype(jnp.bfloat16)

    def attend_prefix(slot):
        half = slot % 2
        for block in range(heads // group):
            rows = slice(block * TILE, (block + 1) * TILE)
            scores = lax.dot_general(
                queries[slot, rows], keys[...], transposed, preferred_element_type=jnp.float32
            )
            scores = scores * score_scale + slot_bias
            peak = jnp.max(scores, axis=-1, keepdims=True)
            weights = jnp.exp2(scores - peak)
            total = jnp.sum(weights, axis=-1, keepdims=True)
            mixes[half, rows] = jnp.dot(
                weights.astype(jnp.bfloat16), values[...], preferred_element_type=jnp.float32
            )
            peaks[half, rows] = jnp.broadcast_to(peak, (TILE, HD))
            totals[half, rows] = jnp.broadcast_to(total, (TILE, HD))

    def attend_span(slot):
        tick, half = slot // 2, slot % 2
        bias = causal_bias[half * HALF : (half + 1) * HALF]
        bias = jnp.concatenate([bias] * group, 0)
        for block in range(heads // group):
            rows = slice(block * TILE, (block + 1) * TILE)
            scores = lax.dot_general(
                queries[slot, rows], span_keys[tick], transposed, preferred_element_type=jnp.float32
            )
            scores = scores * score_scale + bias
            before = peaks[half, rows]
            peak = jnp.maximum(before, jnp.max(scores, axis=-1, keepdims=True))
            weights = jnp.exp2(scores - peak)
            shrink = jnp.exp2(before - peak)
            fresh = jnp.dot(
                weights.astype(jnp.bfloat16), span_values[tick], preferred_element_type=jnp.float32
            )
            total = totals[half, rows] * shrink + jnp.sum(weights, axis=-1, keepdims=True)
            mixed = mixes[half, rows] * shrink + fresh
            mixed = (mixed / total).astype(jnp.bfloat16)
            for place in range(group):
                head = block * group + place
                attended[half * HALF : (half + 1) * HALF, head * HD : (head + 1) * HD] = mixed[
                    place * HALF : (place + 1) * HALF
                ]

    def pass_on(tick, number):
        columns = slice(number * chunk, (number + 1) * chunk)
        pair_copy(tick, number, 1).wait_recv()
        far_send[tick, number] = (
            partial[rows_of(1, core), columns] + pair_recv[tick, number, 1].astype(jnp.float32)
        ).astype(jnp.bfloat16)
        far_copy(tick, number).start()

    def emit(tick, halves):
        first, last = halves[0] * HALF, (halves[-1] + 1) * HALF
        for number in range(OUT_CHUNKS):
            columns = slice(number * chunk, (number + 1) * chunk)
            partial[first:last, columns] = jnp.dot(
                attended[first:last], w_out[:, columns], preferred_element_type=jnp.float32
            )
            for kind in reversed(halves):
                pair_send[tick, number, kind] = partial[rows_of(kind, 1 - core), columns].astype(
                    jnp.bfloat16
                )
                pair_copy(tick, number, kind).start()
            if 1 in halves and number > 1:
                pass_on(tick, number - 2)
        if 1 in halves:
            for number in range(OUT_CHUNKS - 2, OUT_CHUNKS):
                pass_on(tick, number)

    def summed(tick, number):
        columns = slice(number * chunk, (number + 1) * chunk)
        pair_copy(tick, number, 0).wait_recv()
        beside = partial[rows_of(0, core), columns] + pair_recv[tick, number, 0].astype(jnp.float32)
        far_copy(tick, number).wait_recv()
        return (beside + far_recv[tick, number].astype(jnp.float32)).astype(jnp.bfloat16)

    def finish_first(number):
        first_out[number] = summed(0, number)

        @pl.when(has_next)
        def _():
            out_copy(number).start()

    tables(0, index_own[...])
    for part in range(2):
        gather_copy(0, 1, part).wait_recv()
    for load in loads[:5]:
        load.wait()
    project((0,))
    relay_and_shift(0)
    spread((0,))
    for load in loads[5:7]:
        load.wait()
    attend_prefix(0)
    relay_and_shift(1)

    @pl.when(has_prev)
    def _():
        index_copy().wait_recv()

    tables(1, index_in[...])
    for part in range(2):
        gather_copy(0, 2, part).wait_recv()
        gather_copy(1, 1, part).wait_recv()
    project((1, 2))
    spread((1, 2))
    attend_prefix(1)
    attend_span(1)
    attend_span(0)
    for load in loads[7:]:
        load.wait()
    for part in range(2):
        gather_copy(1, 0, part).wait_recv()
        gather_copy(1, 2, part).start()
    emit(0, (0, 1))

    for part in range(2):
        gather_copy(1, 2, part).wait_recv()
    project((3,))
    spread((3,))
    attend_prefix(3)
    attend_span(3)
    for number in range(OUT_CHUNKS // 2):
        finish_first(number)
    emit(1, (1,))
    for number in range(OUT_CHUNKS // 2, OUT_CHUNKS):
        finish_first(number)
    attend_prefix(2)
    attend_span(2)
    emit(1, (0,))
    for number in range(OUT_CHUNKS):
        columns = slice(number * chunk, (number + 1) * chunk)
        output_ref[0, :, columns] = summed(1, number)
    for number in range(OUT_CHUNKS):
        columns = slice(number * chunk, (number + 1) * chunk)

        @pl.when(has_prev)
        def _():
            out_copy(number).wait_recv()

        carried_ref[0, :, columns] = (
            carried_in[:, columns].astype(jnp.float32) + out_in[number].astype(jnp.float32)
        ).astype(jnp.bfloat16)

    for tick in range(2):
        for part in range(2):
            for leg in range(3):
                gather_copy(tick, leg, part).wait_send()
        for number in range(OUT_CHUNKS):
            for kind in range(2):
                pair_copy(tick, number, kind).wait_send()
            far_copy(tick, number).wait_send()

    @pl.when(has_next)
    def _():
        for part in range(2):
            shift_copy(part).wait_send()
        index_copy().wait_send()
        for number in range(OUT_CHUNKS):
            out_copy(number).wait_send()


def hand_out_kernel(carried_from, output_from, carried_to, output_to, sem):
    rows = carried_from.shape[1] // 2
    copies = [
        pltpu.make_async_copy(
            source.at[0, pl.ds(part * rows, rows)],
            target.at[0, pl.ds(part * rows, rows)],
            sem.at[place, part],
        )
        for place, (source, target) in enumerate(
            ((carried_from, carried_to), (output_from, output_to))
        )
        for part in range(2)
    ]
    for copy in copies:
        copy.start()
    for copy in copies:
        copy.wait()


def hand_out(carried, output):
    near = pl.BlockSpec(memory_space=pltpu.VMEM)
    whole = pl.BlockSpec(memory_space=pl.ANY)
    shape = jax.ShapeDtypeStruct(carried.shape, carried.dtype)
    return pl.pallas_call(
        hand_out_kernel,
        out_shape=(shape, shape),
        in_specs=[near, near],
        out_specs=(whole, whole),
        scratch_shapes=[pltpu.SemaphoreType.DMA((2, 2))],
        compiler_params=pltpu.CompilerParams(vmem_limit_bytes=4 * 1024 * 1024),
        name="hand_out",
    )(carried, output)


def fused(
    sections,
    residual,
    pending,
    span_index,
    prefix_len,
    norm_gain,
    w_query,
    w_kv,
    w_out,
    prefix_cache,
):
    features, query_width = w_query.shape[1:]
    pair_width = w_kv.shape[2]
    chunk = features // OUT_CHUNKS
    smem = pl.BlockSpec(memory_space=pltpu.SMEM)
    vmem = pl.BlockSpec(memory_space=pltpu.VMEM)
    whole = pl.BlockSpec(memory_space=pl.ANY)
    half = jnp.bfloat16
    dma = pltpu.SemaphoreType.DMA
    carried, output = pl.pallas_call(
        functools.partial(fused_kernel, sections),
        out_shape=(
            jax.ShapeDtypeStruct(residual.shape, half),
            jax.ShapeDtypeStruct(residual.shape, half),
        ),
        in_specs=[smem, smem] + [whole] * 7,
        out_specs=(vmem, vmem),
        scratch_shapes=[
            pltpu.VMEM((ROWS, features), half),
            pltpu.VMEM((ROWS, features), half),
            pltpu.VMEM((1, features), half),
            pltpu.VMEM((features, query_width), half),
            pltpu.VMEM((features, pair_width), half),
            pltpu.VMEM((query_width, features), half),
            pltpu.VMEM((PREFIX, HD), half),
            pltpu.VMEM((PREFIX, HD), half),
            pltpu.VMEM((2, SPAN, HD), half),
            pltpu.VMEM((2, SPAN, HD), half),
            pltpu.VMEM((2 * SPAN, features), half),
            pltpu.VMEM((ROWS, features), half),
            pltpu.VMEM((ROWS, features), half),
            pltpu.VMEM((8, HD), jnp.int32),
            pltpu.VMEM((8, HD), jnp.int32),
            pltpu.VMEM((2, SPAN, HD), jnp.float32),
            pltpu.VMEM((2, SPAN, HD), jnp.float32),
            pltpu.VMEM((SPAN, query_width + pair_width), jnp.float32),
            pltpu.VMEM((4, query_width // HD * HALF, HD), half),
            pltpu.VMEM((2, query_width // HD * HALF, HD), jnp.float32),
            pltpu.VMEM((2, query_width // HD * HALF, HD), jnp.float32),
            pltpu.VMEM((2, query_width // HD * HALF, HD), jnp.float32),
            pltpu.VMEM((SPAN, query_width), half),
            pltpu.VMEM((SPAN, features), jnp.float32),
            pltpu.VMEM((2, OUT_CHUNKS, 2, ROWS, chunk), half),
            pltpu.VMEM((2, OUT_CHUNKS, 2, ROWS, chunk), half),
            pltpu.VMEM((2, OUT_CHUNKS, ROWS, chunk), half),
            pltpu.VMEM((2, OUT_CHUNKS, ROWS, chunk), half),
            pltpu.VMEM((OUT_CHUNKS, ROWS, chunk), half),
            pltpu.VMEM((OUT_CHUNKS, ROWS, chunk), half),
            dma((3,)),
            dma((11,)),
            dma((2, 3, 2)),
            dma((2, 3, 2)),
            dma((3,)),
            dma((3,)),
            dma((2, OUT_CHUNKS, 2)),
            dma((2, OUT_CHUNKS, 2)),
            dma((2, OUT_CHUNKS)),
            dma((2, OUT_CHUNKS)),
            dma((OUT_CHUNKS,)),
            dma((OUT_CHUNKS,)),
        ],
        compiler_params=pltpu.CompilerParams(
            collective_id=0, has_side_effects=True, vmem_limit_bytes=54528 * 1024
        ),
        name="fused_relay",
    )(
        span_index,
        prefix_len,
        residual,
        pending,
        norm_gain,
        w_query,
        w_kv,
        w_out,
        prefix_cache,
    )
    return hand_out(carried, output)


def solution(mesh):
    in_specs = (
        P("segment", "tp", None),
        P("segment", "tp", None),
        P("segment"),
        P("segment"),
        P("segment", None),
        P("segment", None, "tp"),
        P("segment", None, "tp"),
        P("segment", "tp", None),
        P("segment", "tp", None),
    )
    out_specs = (P("segment", "tp", None), P("segment", "tp", None))
    body = shards
    if mesh.shape["tp"] == TP == KV_HEADS and TICKS == 2:
        body = functools.partial(fused, mesh.shape["segment"])
    return jax.shard_map(body, mesh=mesh, in_specs=in_specs, out_specs=out_specs, check_vma=False)
```
